128 devices in a mesh: site: 32 (over z, x, core), band: 4 (over y).
Axes of the slice: x: 4, y: 4, z: 4, core: 2. Of those that a mesh axis runs over, the one named last changes fastest.
Arguments:
- fields: bfloat16 [4096, 32, 4096], P('site', None, 'band'), may hold values from -6 to 6
- factor: bfloat16 [4096, 4, 128], P('site'), may hold values from -0.25 to 0.25
- pattern: int32 [32, 3], P('site'), may hold values 0 or 1
- tx_power: float32 [4096], replicated, may hold values from 30 to 49
- site_position: float32 [2, 4096], replicated, may hold values from 0 to 1, as said below
- candidates: int32 [32, 16], P('site'), may hold values from 0 to 4095, as said below
Outputs:
- best_level: float32 [32, 4096], P('site', 'band')
- sinr_level: float32 [32, 4096], P('site', 'band')
- tile_mean: float32 [32], P('site')
The draws below stay inside these ranges and needn't reach their ends.
Inputs may be any that keep to these rules, and one draw needn't show every extreme that they name: `site_position`: tile t covers column t % 8 and row t // 8 of a grid of 8 x (4) tiles over the window. Site s lies in tile s // 128, which is cut into 16 columns by 8 rows of equal cells, each holding exactly one of the tile's sites. The candidates of tile t are its 16 sites in the top row of cells, in order of cell column; they are distinct.
All inputs are finite; a program needn't handle non-finite values. No bound on the sum of `pattern` on one device may be relied on, other than what follows from the above.
Results may differ from the reference program's by a relative error of at most 0.005.
Values may be sent and summed in bfloat16 or wider, within the bound.
A program may use at most 192 MiB of HBM per device.

```python
import jax
import jax.numpy as jnp
from jax import lax

SITE_DEV = 128
SITES = 4096
TILES = 32
ROWS = 16
COLS = 256
DEPTH = 4
CAND = 16
N_SITE = 32


def cell_of_site(key):
    keys = jax.random.split(jax.random.fold_in(key, 11), TILES)
    return jax.vmap(lambda single: jax.random.permutation(single, SITE_DEV))(keys).astype(jnp.int32)


def draw_candidates(key, part):
    cells = cell_of_site(key)
    occupant = jnp.argsort(cells, axis=1, stable=True).astype(jnp.int32)
    tile_base = (jnp.arange(TILES, dtype=jnp.int32) * SITE_DEV)[:, None]
    return (tile_base + occupant[:, :CAND]).astype(jnp.int32)


def draw_site_position(key, part):
    cells = cell_of_site(key)
    cell_col = (cells % CAND).astype(jnp.float32)
    cell_row = (cells // CAND).astype(jnp.float32)
    rows_per = float(SITE_DEV // CAND)
    height = float(TILES // 8)
    tile_index = jnp.arange(TILES, dtype=jnp.int32)[:, None]
    tile_col = (tile_index % 8).astype(jnp.float32)
    tile_row = (tile_index // 8).astype(jnp.float32)
    jitter = jax.random.uniform(jax.random.fold_in(key, 12), (2, TILES, SITE_DEV), jnp.float32)
    pos_x = (tile_col + (cell_col + jitter[0]) / float(CAND)) / 8.0
    pos_y = (tile_row + (cell_row + jitter[1]) / rows_per) / height
    both = jnp.stack([pos_x.reshape(SITES), pos_y.reshape(SITES)], axis=0)
    return jnp.clip(both, 0.0, 1.0).astype(jnp.float32)


def place_ends(array, key, low, top_value):
    longest = array.shape.index(max(array.shape))
    spots = []
    for shift in (0, 1):
        where = [jax.random.randint(jax.random.fold_in(key, axis), (), 0, length) for axis, length in enumerate(array.shape)]
        where[longest] = (where[longest] + shift) % array.shape[longest]
        spots.append(tuple(where))
    return array.at[spots[0]].set(low).at[spots[1]].set(top_value)


def shard_levels(key, dims, cuts, least, top_value):
    level, own = 1.0, jax.random.fold_in(key, 6)
    for dim, blocks in cuts:
        heights = jnp.exp(jax.random.uniform(jax.random.fold_in(own, dim), (blocks,), jnp.float32, least / len(cuts), top_value / len(cuts)))
        level = level * jnp.repeat(heights, dims[dim] // blocks).reshape([-1 if axis == dim else 1 for axis in range(len(dims))])
    return level


def gaussian(stream_key, shape, scale, reach, cuts=(), kind=jnp.bfloat16):
    level = shard_levels(stream_key, shape, cuts, -0.22, 0.18) if cuts else 1.0
    result = jax.random.normal(stream_key, shape, jnp.float32) * scale * level
    return jnp.minimum(jnp.maximum(result, -reach), reach).astype(kind)


def setup_inputs(seed: int = 0) -> dict:
    streams_of = jax.random.split(jax.random.key(seed), 7)
    fields = gaussian(streams_of[0], (SITES, TILES, ROWS * COLS), 1.0, 6.0, ((0, 32), (2, 4)))
    factor = gaussian(streams_of[1], (SITES, DEPTH, SITE_DEV), (DEPTH * SITE_DEV) ** -0.5, 0.25, ((0, 32),))
    pattern = place_ends((jax.random.randint(streams_of[2], (N_SITE, DEPTH - 1), 0, 3) < 2).astype(jnp.int32), jax.random.fold_in(streams_of[2], 1), 0, 1)
    tx_power = jnp.clip(jax.random.uniform(streams_of[3], (SITES,), jnp.float32, 30.0, 49.0), 30.0, 49.0)
    site_position = draw_site_position(jax.random.fold_in(streams_of[6], 71), 0)
    candidates = draw_candidates(jax.random.fold_in(streams_of[6], 71), 0)
    return dict(fields=fields, factor=factor, pattern=pattern, tx_power=tx_power, site_position=site_position, candidates=candidates)


spacing = 0.03
ln_tenth = 0.2302585093

def coverage(mixed, tile_number, row_start, row_count, height, tx_power, site_position, cand_row):
    pixel = jnp.arange(row_count * COLS, dtype=jnp.int32)
    row_index = row_start + pixel // COLS
    col_index = pixel % COLS
    pos_x = (tile_number % 8 * COLS + col_index).astype(jnp.float32) * spacing
    pos_y = (tile_number // 8 * COLS + row_index).astype(jnp.float32) * spacing
    site_x = site_position[0] * (8.0 * COLS * spacing)
    site_y = site_position[1] * (height * COLS * spacing)
    dist = jnp.sqrt((site_x[:, None] - pos_x[None, :]) ** 2 + (site_y[:, None] - pos_y[None, :]) ** 2 + spacing * spacing)
    level = tx_power[:, None] - (100.0 + 22.0 * jnp.log10(dist)) + 8.0 * mixed.astype(jnp.float32) + 90.0
    power = jnp.exp(ln_tenth * level)
    cand_power = jnp.take(power, cand_row, axis=0)
    best = lax.optimization_barrier(jnp.max(cand_power, axis=0))
    serving = jnp.take(cand_row, jnp.argmax(cand_power, axis=0).astype(jnp.int32))
    site_ids = jnp.arange(power.shape[0], dtype=jnp.int32)
    interference = lax.optimization_barrier(jnp.sum(jnp.where(site_ids[:, None] == serving[None, :], 0.0, power), axis=0))
    return (jnp.log10(best), jnp.log10(best / interference))

def reference(fields, factor, pattern, tx_power, site_position, candidates):
    nblocks = SITES // SITE_DEV
    pixels = ROWS * COLS
    blocks = fields.reshape(nblocks, SITE_DEV, TILES, pixels)
    lower = jnp.tril(jnp.ones((SITE_DEV, SITE_DEV), jnp.float32))

    def one_tile(tile_number):
        tile_fields = jnp.take(blocks, tile_number, axis=2)
        total = jnp.zeros((nblocks, SITE_DEV, pixels), jnp.float32)
        for offset in range(DEPTH):
            shifted = jnp.concatenate([jnp.zeros((offset, SITE_DEV, pixels), jnp.bfloat16), tile_fields[:nblocks - offset]], axis=0)
            coef = factor[:, offset, :].reshape(nblocks, SITE_DEV, SITE_DEV).astype(jnp.float32)
            if offset == 0:
                coef = coef * lower
            else:
                coef = coef * pattern[:, offset - 1].astype(jnp.float32)[:, None, None]
            total = total + jnp.einsum('nik,nkp->nip', coef, shifted.astype(jnp.float32), precision=lax.Precision.HIGHEST)
        mixed = total.astype(jnp.bfloat16).reshape(SITES, pixels)
        cand_row = jnp.take(candidates, tile_number, axis=0)
        return coverage(mixed, tile_number, 0, ROWS, TILES // 8, tx_power, site_position, cand_row)
    best_level, sinr_level = lax.map(one_tile, jnp.arange(TILES, dtype=jnp.int32))
    tile_mean = lax.optimization_barrier(jnp.mean(sinr_level, axis=1))
    return (best_level, sinr_level, tile_mean)
```

```python
import functools
import math

import jax
import jax.numpy as jnp
from jax import lax
from jax.experimental import pallas as pl
from jax.experimental.pallas import tpu as pltpu
from jax.sharding import PartitionSpec as P

MESH = pl.DeviceIdType.MESH
COLS = 256
SPACING = 0.03
CUTS = 4
PARTS = 2 * CUTS
BLOCK = 128
HALO = 3
ROW = 8
DB = math.log2(10.0) / 10.0
FIELD_GAIN = 8.0 * DB
NOTHING = -1e30
PEERS = ((0, 1), (1, 0), (3, 0), (1, 1), (3, 1), (2, 0), (2, 1))


def kernel(
    fields, weights, cand, tx, pos,
    best_out, sinr_out, mean_out,
    land, halo, mixed_in, loss, cand_loss, wbuf, site_x, site_y, site_a, cbuf,
    acc, tot, zred, msg, rows, msum, means,
    send_sem, recv_sem, zs, zr, w_send, w_recv, w2_send, w2_recv, c_send, c_recv,
    t_send, t_recv, o_send, o_recv, m_send, m_recv,
):
    site = lax.axis_index("site")
    band = lax.axis_index("band")
    z = site // 8
    j = site % 8
    x = j // 2
    c = j % 2
    cut = BLOCK // CUTS

    def at_row(dx, dc):
        return ((x + dx) % 4) * 2 + (c + dc) % 2

    barrier = pltpu.get_barrier_semaphore()
    count = 0
    for dx, dc in PEERS:
        pl.semaphore_signal(barrier, inc=1, device_id=(z * 8 + at_row(dx, dc), band), device_id_type=MESH)
        count += 1
    for dz in (1, 2, 3):
        pl.semaphore_signal(barrier, inc=1, device_id=(((z + dz) % 4) * 8 + j, band), device_id_type=MESH)
        count += 1
    for dy in (1, 2, 3):
        for dc in (0, 1):
            pl.semaphore_signal(
                barrier, inc=1, device_id=(z * 8 + at_row(0, dc), (band + dy) % 4), device_id_type=MESH
            )
            count += 1
    pl.semaphore_wait(barrier, count)

    def remote(src, dst, send, recv, to_site, to_band):
        return pltpu.make_async_remote_copy(
            src_ref=src, dst_ref=dst, send_sem=send, recv_sem=recv,
            device_id=(to_site, to_band), device_id_type=MESH,
        )

    quarter = pl.ds(pl.multiple_of(band * 32, 32), 32)

    def w_copy(dx):
        return remote(
            weights.at[quarter], wbuf.at[c, x, quarter], w_send.at[dx], w_recv.at[x],
            z * 8 + at_row(dx, 0), band,
        )

    def w2_copy(dc, dy):
        mine = wbuf.at[c, :, quarter]
        return remote(
            mine, mine, w2_send.at[dc * 4 + dy], w2_recv.at[c * 4 + band],
            z * 8 + at_row(0, dc), (band + dy) % 4,
        )

    def c_copy(q):
        dx, dc = PEERS[q]
        return remote(cand, cbuf.at[j], c_send.at[q], c_recv.at[j], z * 8 + at_row(dx, dc), band)

    w_own = pltpu.make_async_copy(weights.at[quarter], wbuf.at[c, x, quarter], w_recv.at[x])
    w_own.start()
    c_own = pltpu.make_async_copy(cand, cbuf.at[j], c_recv.at[j])
    c_own.start()
    for dx in (1, 2, 3):
        w_copy(dx).start()
    for q in range(7):
        c_copy(q).start()

    def piece(p):
        return pl.ds((p % CUTS) * cut, cut), pl.ds((p // CUTS) * 16, 16)

    def chunk(owner, p):
        sites, tiles = piece(p)
        return fields.at[sites, tiles, pl.ds(pl.multiple_of(owner * 128, 128), 128)]

    def landed(block, p):
        sites, tiles = piece(p)
        return land.at[block, sites, tiles]

    def send(q, p):
        dx, dc = PEERS[q]
        owner = at_row(dx, dc)
        return remote(
            chunk(owner, p), landed(j, p), send_sem.at[q * PARTS + p], recv_sem.at[j * PARTS + p],
            z * 8 + owner, band,
        )

    def forward(h, p):
        sites, tiles = piece(p)
        return remote(
            landed(ROW - HALO + h, p), halo.at[h, sites, tiles], zs.at[h * PARTS + p], zr.at[h * PARTS + p],
            ((z + 1) % 4) * 8 + j, band,
        )

    for p in range(PARTS):
        pltpu.make_async_copy(chunk(j, p), landed(j, p), recv_sem.at[j * PARTS + p]).start()
    for p in range(PARTS):
        for q in range(7):
            send(q, p).start()

    def arrived(block, p):
        ref = landed(block, p)
        pltpu.make_async_copy(ref, ref, recv_sem.at[block * PARTS + p]).wait()

    eight = pl.ds(pl.multiple_of(z * 8, 8), 8)
    xs_rows = pos[0, eight, :] * (8.0 * COLS * SPACING)
    ys_rows = pos[1, eight, :] * (4.0 * COLS * SPACING)
    tx_rows = (tx[eight, :] - 10.0) * DB
    for b in range(ROW):
        for ref, values in ((site_x, xs_rows), (site_y, ys_rows), (site_a, tx_rows)):
            ref[b] = jnp.transpose(jnp.broadcast_to(values[b : b + 1, :], (BLOCK, BLOCK)))

    lane = lax.broadcasted_iota(jnp.int32, (1, 128), 1)
    column = (j % 2) * 128 + lane
    pixel_row = band * 4 + j // 2

    def path_loss(b):
        @pl.loop(0, 16)
        def _(pair):
            for u in range(2):
                tile = pair * 2 + u
                px = ((tile % 8) * COLS + column).astype(jnp.float32) * SPACING
                py = ((tile // 8) * COLS + pixel_row).astype(jnp.float32) * SPACING
                dx = site_x[b] - px
                dy = site_y[b] - py
                d2 = dx * dx + dy * dy + SPACING * SPACING
                loss[pair, b * BLOCK : (b + 1) * BLOCK, u * 128 : (u + 1) * 128] = (
                    site_a[b] - (1.1 / math.log(2.0)) * jnp.log(d2)
                )

    def split_candidates():
        for b in range(ROW):
            ids = jnp.broadcast_to(cbuf[b, 0:1, :], (BLOCK, BLOCK))
            place = lax.broadcasted_iota(jnp.int32, (BLOCK, BLOCK), 0).astype(jnp.float32)
            hit = jnp.max(jnp.where(ids == place, 1.0, 0.0), axis=1, keepdims=True)
            is_cand = jnp.broadcast_to(hit, (BLOCK, BLOCK)) > 0.5
            where = (z * 4 + b // 2, slice(b * BLOCK, (b + 1) * BLOCK), slice((b % 2) * 128, (b % 2) * 128 + 128))
            level = loss[where]
            cand_loss[b] = jnp.where(is_cand, level, NOTHING)
            loss[where] = jnp.where(is_cand, NOTHING, level)

    def turn(source, block, p, row):
        first, half = (p % CUTS) * cut, p // CUTS
        values = source[block, first : first + cut, half * 16 : half * 16 + 16, :].astype(jnp.float32)
        turned = jnp.transpose(values, (1, 0, 2)).astype(jnp.bfloat16)
        for t in range(16):
            mixed_in[
                half * 8 + t // 2,
                pl.ds(pl.multiple_of(row * BLOCK + first, cut), cut),
                (t % 2) * 128 : (t % 2) * 128 + 128,
            ] = turned[t]

    def mix(half, b):
        w = wbuf[b % 2, b // 2]

        @pl.loop(0, 8)
        def _(step):
            pair = half * 8 + step
            fresh = mixed_in[pair, b * BLOCK : (b + 4) * BLOCK, :]
            mixed = jnp.dot(w, fresh, preferred_element_type=jnp.float32)
            power = jnp.exp2(loss[pair, b * BLOCK : (b + 1) * BLOCK, :] + FIELD_GAIN * mixed)
            acc[pair] += jnp.sum(power.reshape(BLOCK // 8, 8, 256), axis=0)

    acc[...] = jnp.zeros_like(acc)

    @pl.when(z == 0)
    def _():
        mixed_in[:, 0 : HALO * BLOCK, :] = jnp.zeros((16, HALO * BLOCK, 256), jnp.bfloat16)

    def halo_in(p):
        @pl.when(z > 0)
        def _():
            for h in range(HALO):
                forward(h, p).wait_recv()
                turn(halo, h, p, h)

    for p in range(PARTS):
        for h in (1, 2, 0):
            arrived(ROW - HALO + h, p)

            @pl.when(z < 3)
            def _():
                forward(h, p).start()

        if p < 4:
            path_loss(2 * p)
            path_loss(2 * p + 1)
        if p == 0:
            for dx in (1, 2, 3):
                other = (x + dx) % 4
                got = wbuf.at[c, other, quarter]
                pltpu.make_async_copy(got, got, w_recv.at[other]).wait()
            w_own.wait()
            for dc in (0, 1):
                for dy in range(4):
                    if dc or dy:
                        w2_copy(dc, dy).start()
        if p == 1:
            for b in range(ROW):
                pltpu.make_async_copy(cbuf.at[b], cbuf.at[b], c_recv.at[b]).wait()
            for dc in (0, 1):
                for dy in range(4):
                    if dc or dy:
                        other_c, other_y = (c + dc) % 2, (band + dy) % 4
                        got = wbuf.at[other_c, :, pl.ds(pl.multiple_of(other_y * 32, 32), 32)]
                        pltpu.make_async_copy(got, got, w2_recv.at[other_c * 4 + other_y]).wait()
        if p == 3:
            split_candidates()
        for b in range(ROW):
            if b < ROW - HALO:
                arrived(b, p)
            turn(land, b, p, b + HALO)
        if p == CUTS - 1:
            for b in range(HALO, ROW):
                mix(0, b)
        if p == CUTS + 1:
            for k in range(CUTS):
                halo_in(k)
        if p == CUTS + 2:
            for b in range(HALO):
                mix(0, b)
    for b in range(HALO, ROW):
        mix(1, b)
    for k in range(CUTS):
        halo_in(CUTS + k)
    for b in range(HALO):
        mix(1, b)

    for pair in range(16):
        both = jnp.sum(acc[pair], axis=0, keepdims=True)
        tot[2 * pair : 2 * pair + 1, :] = both[:, :128]
        tot[2 * pair + 1 : 2 * pair + 2, :] = both[:, 128:]

    def t_copy(dz):
        to = (z + dz) % 4
        return remote(
            tot.at[pl.ds(pl.multiple_of(to * 8, 8), 8)], zred.at[z], t_send.at[dz], t_recv.at[z], to * 8 + j, band
        )

    for dz in (1, 2, 3):
        t_copy(dz).start()

    bests, rests = [], []
    for b in range(ROW):
        lanes = slice((b % 2) * 128, (b % 2) * 128 + 128)
        fresh = mixed_in[z * 4 + b // 2, b * BLOCK : (b + 4) * BLOCK, lanes]
        mixed = jnp.dot(wbuf[b % 2, b // 2], fresh, preferred_element_type=jnp.float32)
        level = cand_loss[b]
        power = jnp.exp2(level + FIELD_GAIN * mixed)
        best = jnp.max(power, axis=0, keepdims=True)
        serves = (power == best) & (level > 0.5 * NOTHING)
        ties = jnp.sum(jnp.where(serves, 1.0, 0.0), axis=0, keepdims=True)
        rest = jnp.sum(jnp.where(serves, 0.0, power), axis=0, keepdims=True)
        bests.append(best)
        rests.append(rest + jnp.where(ties > 1.5, (ties - 1.0) * best, 0.0))
    best = jnp.concatenate(bests, axis=0)
    others = jnp.concatenate(rests, axis=0) + tot[eight, :]
    for dz in (1, 2, 3):
        came = (z + dz) % 4
        pltpu.make_async_copy(zred.at[came], zred.at[came], t_recv.at[came]).wait()
        others = others + zred[came]
    to_log10 = 1.0 / math.log(10.0)
    best_level = jnp.log(best) * to_log10
    sinr_level = jnp.log(best / others) * to_log10
    for b in range(ROW):
        msg[b, 0:1, :] = best_level[b : b + 1, :]
        msg[b, 1:2, :] = sinr_level[b : b + 1, :]

    def o_copy(q):
        owner = at_row(*PEERS[q])
        return remote(msg.at[owner], rows.at[j], o_send.at[q], o_recv.at[j], z * 8 + owner, band)

    for q in range(7):
        o_copy(q).start()
    rows[j] = msg[j]
    for q in range(7):
        came = at_row(*PEERS[q])
        pltpu.make_async_copy(rows.at[came], rows.at[came], o_recv.at[came]).wait()
    total = rows[0, 1:2, :]
    for k in range(1, ROW):
        total = total + rows[k, 1:2, :]
    msum[...] = jnp.broadcast_to(total, (8, 128))

    def m_copy(dy):
        return remote(msum, means.at[band], m_send.at[dy], m_recv.at[band], site, (band + dy) % 4)

    for dy in (1, 2, 3):
        m_copy(dy).start()
    means[band] = msum[...]
    for k in range(ROW):
        best_out[:, k * 128 : (k + 1) * 128] = rows[k, 0:1, :]
        sinr_out[:, k * 128 : (k + 1) * 128] = rows[k, 1:2, :]
    for dy in (1, 2, 3):
        came = (band + dy) % 4
        pltpu.make_async_copy(means.at[came], means.at[came], m_recv.at[came]).wait()
    total = (means[0] + means[1]) + (means[2] + means[3])
    mean = jnp.sum(total, axis=1, keepdims=True) * (1.0 / 4096.0)
    mean_out[...] = jnp.broadcast_to(mean, (8, 128))

    for q in range(7):
        c_copy(q).wait_send()
        o_copy(q).wait_send()
        for p in range(PARTS):
            send(q, p).wait_send()
    for dx in (1, 2, 3):
        w_copy(dx).wait_send()
        t_copy(dx).wait_send()
        m_copy(dx).wait_send()
    for dc in (0, 1):
        for dy in range(4):
            if dc or dy:
                w2_copy(dc, dy).wait_send()

    @pl.when(z < 3)
    def _():
        for h in range(HALO):
            for p in range(PARTS):
                forward(h, p).wait_send()


def shards(fields, factor, pattern, tx_power, site_position, candidates):
    block = fields.shape[0]
    lower = jnp.tril(jnp.ones((block, block), jnp.bfloat16))
    columns = [
        factor[:, d, :] * pattern[0, d - 1].astype(jnp.bfloat16) for d in (3, 2, 1)
    ] + [factor[:, 0, :] * lower]
    weights = jnp.concatenate(columns, axis=1)
    local = (candidates - lax.axis_index("site") * block).astype(jnp.float32)
    cand = jnp.broadcast_to(jnp.pad(local, ((0, 0), (0, 128 - local.shape[1])), constant_values=-1.0), (8, 128))
    dma = pltpu.SemaphoreType.DMA
    f32, bf16 = jnp.float32, jnp.bfloat16
    vmem = pl.BlockSpec(memory_space=pltpu.VMEM)
    best, sinr, mean = pl.pallas_call(
        kernel,
        out_shape=(
            jax.ShapeDtypeStruct((1, 1024), f32),
            jax.ShapeDtypeStruct((1, 1024), f32),
            jax.ShapeDtypeStruct((8, 128), f32),
        ),
        in_specs=[pl.BlockSpec(memory_space=pl.ANY), vmem, vmem, vmem, vmem],
        out_specs=(vmem, vmem, vmem),
        scratch_shapes=[
            pltpu.VMEM((ROW, BLOCK, 32, 128), bf16),
            pltpu.VMEM((HALO, BLOCK, 32, 128), bf16),
            pltpu.VMEM((16, (HALO + ROW) * BLOCK, 256), bf16),
            pltpu.VMEM((16, ROW * BLOCK, 256), f32),
            pltpu.VMEM((ROW, BLOCK, 128), f32),
            pltpu.VMEM((2, 4, BLOCK, 512), bf16),
            pltpu.VMEM((ROW, BLOCK, 128), f32),
            pltpu.VMEM((ROW, BLOCK, 128), f32),
            pltpu.VMEM((ROW, BLOCK, 128), f32),
            pltpu.VMEM((ROW, 8, 128), f32),
            pltpu.VMEM((16, 8, 256), f32),
            pltpu.VMEM((32, 128), f32),
            pltpu.VMEM((4, 8, 128), f32),
            pltpu.VMEM((ROW, 8, 128), f32),
            pltpu.VMEM((ROW, 8, 128), f32),
            pltpu.VMEM((8, 128), f32),
            pltpu.VMEM((4, 8, 128), f32),
            dma((7 * PARTS,)), dma((8 * PARTS,)), dma((HALO * PARTS,)), dma((HALO * PARTS,)),
            dma((4,)), dma((4,)), dma((8,)), dma((8,)), dma((7,)), dma((8,)),
            dma((4,)), dma((4,)), dma((7,)), dma((8,)), dma((4,)), dma((4,)),
        ],
        compiler_params=pltpu.CompilerParams(
            collective_id=0, has_side_effects=True, vmem_limit_bytes=56 << 20
        ),
    )(fields, weights, cand, tx_power.reshape(32, 128), site_position.reshape(2, 32, 128))
    return (best, sinr, mean[0, 0:1])


def solution(mesh):
    placed = (
        P("site", None, "band"),
        P("site", None, None),
        P("site", None),
        P(),
        P(),
        P("site", None),
    )
    return jax.shard_map(
        shards,
        mesh=mesh,
        in_specs=placed,
        out_specs=(P("site", "band"), P("site", "band"), P("site")),
        check_vma=False,
    )
```

```python
import functools
import math

import jax
import jax.numpy as jnp
from jax import lax
from jax.experimental import pallas as pl
from jax.experimental.pallas import tpu as pltpu
from jax.sharding import PartitionSpec as P

MESH = pl.DeviceIdType.MESH
COLS = 256
SPACING = 0.03
PIECES = (
    (0, 0, 32), (0, 32, 32), (0, 64, 64),
    (1, 0, 32), (1, 32, 32), (1, 64, 32), (1, 96, 16), (1, 112, 16),
)
PARTS = len(PIECES)
HELD = 2
BLOCK = 128
HALO = 3
ROW = 8
DB = math.log2(10.0) / 10.0
FIELD_GAIN = 8.0 * DB
NOTHING = -1e30
PEERS = ((0, 1), (1, 0), (3, 0), (1, 1), (3, 1), (2, 0), (2, 1))


def kernel(
    fields, factor, pattern, tx_power, site_position, candidates,
    out,
    factor_in, pattern_in, tx, pos, cand_in,
    land, halo, mixed_in, loss, cand_loss, wbuf, site_x, site_y, site_a, cbuf,
    acc, rows, msum, means,
    send_sem, recv_sem, zs, zr, w_send, w_recv, w2_send, w2_recv, c_send, c_recv,
    o_send, o_recv, m_send, m_recv, local,
):
    site = lax.axis_index("site")
    band = lax.axis_index("band")
    z = site // 8
    j = site % 8
    x = j // 2
    c = j % 2
    quarter = pl.ds(pl.multiple_of(band * 32, 32), 32)
    row_sites = pl.ds(pl.multiple_of(z * 1024, 1024), 1024)
    small = [
        pltpu.make_async_copy(factor.at[quarter], factor_in, local.at[0]),
        pltpu.make_async_copy(pattern, pattern_in, local.at[1]),
        pltpu.make_async_copy(tx_power.at[:, row_sites], tx, local.at[2]),
        pltpu.make_async_copy(site_position.at[:, row_sites], pos, local.at[3]),
        pltpu.make_async_copy(candidates, cand_in, local.at[4]),
    ]
    for copy in small:
        copy.start()

    def at_row(dx, dc):
        return ((x + dx) % 4) * 2 + (c + dc) % 2

    barrier = pltpu.get_barrier_semaphore()
    count = 0
    for dz in range(4):
        for dx, dc in PEERS + (((0, 0),) if dz else ()):
            to = ((z + dz) % 4) * 8 + at_row(dx, dc)
            pl.semaphore_signal(barrier, inc=1, device_id=(to, band), device_id_type=MESH)
            count += 1
    for dy in (1, 2, 3):
        for dc in (0, 1):
            pl.semaphore_signal(
                barrier, inc=1, device_id=(z * 8 + at_row(0, dc), (band + dy) % 4), device_id_type=MESH
            )
            count += 1
    pl.semaphore_wait(barrier, count)

    def remote(src, dst, send, recv, to_site, to_band):
        return pltpu.make_async_remote_copy(
            src_ref=src, dst_ref=dst, send_sem=send, recv_sem=recv,
            device_id=(to_site, to_band), device_id_type=MESH,
        )

    def w_copy(dx):
        mine = wbuf.at[c, x, quarter]
        return remote(mine, mine, w_send.at[dx], w_recv.at[x], z * 8 + at_row(dx, 0), band)

    def w2_copy(dc, dy):
        mine = wbuf.at[c, :, quarter]
        return remote(
            mine, mine, w2_send.at[dc * 4 + dy], w2_recv.at[c * 4 + band],
            z * 8 + at_row(0, dc), (band + dy) % 4,
        )

    def c_copy(q):
        dx, dc = PEERS[q]
        return remote(cbuf.at[j], cbuf.at[j], c_send.at[q], c_recv.at[j], z * 8 + at_row(dx, dc), band)

    def piece(p):
        half, first, count = PIECES[p]
        return pl.ds(first, count), pl.ds(half * 16, 16)

    def chunk(owner, p):
        sites, tiles = piece(p)
        return fields.at[sites, tiles, pl.ds(pl.multiple_of(owner * 128, 128), 128)]

    def landed(block, p):
        sites, tiles = piece(p)
        return land.at[block, sites, tiles]

    def send(q, p):
        dx, dc = PEERS[q]
        owner = at_row(dx, dc)
        return remote(
            chunk(owner, p), landed(j, p), send_sem.at[q * PARTS + p], recv_sem.at[j * PARTS + p],
            z * 8 + owner, band,
        )

    def forward(h, p):
        sites, tiles = piece(p)
        return remote(
            landed(ROW - HALO + h, p), halo.at[h, sites, tiles], zs.at[h * PARTS + p], zr.at[h * PARTS + p],
            ((z + 1) % 4) * 8 + j, band,
        )

    for p in range(PARTS):
        pltpu.make_async_copy(chunk(j, p), landed(j, p), recv_sem.at[j * PARTS + p]).start()
    for q in range(7):
        send(q, 0).start()
    for copy in small:
        copy.wait()
    site_row = lax.broadcasted_iota(jnp.int32, (32, BLOCK), 0) + band * 32
    site_column = lax.broadcasted_iota(jnp.int32, (32, BLOCK), 1)
    for d in range(4):
        rows_of = factor_in[:, d, :].astype(jnp.float32)
        if d == 0:
            kept = jnp.where(site_column <= site_row, rows_of, 0.0)
        else:
            present = pattern_in[0:1, d - 1 : d].astype(jnp.float32)
            kept = rows_of * jnp.broadcast_to(present, (32, BLOCK))
        wbuf[c, x, quarter, (3 - d) * BLOCK : (4 - d) * BLOCK] = kept.astype(jnp.bfloat16)
    cbuf[j] = jnp.full((8, 128), -1.0, jnp.float32)
    cbuf[j, 0:1, 0:16] = (cand_in[...] - site * BLOCK).astype(jnp.float32)
    for dx in (1, 2, 3):
        w_copy(dx).start()
    for q in range(7):
        c_copy(q).start()
    for p in range(1, PARTS - HELD):
        for q in range(7):
            send(q, p).start()
    if HELD:
        @pl.when(j >= ROW - HALO)
        def _():
            for p in range(PARTS - HELD, PARTS):
                for q in range(7):
                    send(q, p).start()

    def arrived(block, p):
        ref = landed(block, p)
        pltpu.make_async_copy(ref, ref, recv_sem.at[block * PARTS + p]).wait()

    eight = pl.ds(pl.multiple_of(z * 8, 8), 8)
    for b in range(ROW):
        block = slice(b * BLOCK, (b + 1) * BLOCK)
        xs = pos[0:1, block] * (8.0 * COLS * SPACING)
        ys = pos[1:2, block] * (4.0 * COLS * SPACING)
        level = (tx[0:1, block] - 10.0) * DB
        for ref, values in ((site_x, xs), (site_y, ys), (site_a, level)):
            ref[b] = jnp.transpose(jnp.broadcast_to(values, (BLOCK, BLOCK)))

    lane = lax.broadcasted_iota(jnp.int32, (1, 128), 1)
    column = (j % 2) * 128 + lane
    pixel_row = band * 4 + j // 2

    def path_loss(b):
        @pl.loop(0, 16)
        def _(pair):
            for u in range(2):
                tile = pair * 2 + u
                px = ((tile % 8) * COLS + column).astype(jnp.float32) * SPACING
                py = ((tile // 8) * COLS + pixel_row).astype(jnp.float32) * SPACING
                dx = site_x[b] - px
                dy = site_y[b] - py
                d2 = dx * dx + dy * dy + SPACING * SPACING
                loss[pair, b * BLOCK : (b + 1) * BLOCK, u * 128 : (u + 1) * 128] = (
                    site_a[b] - (1.1 / math.log(2.0)) * jnp.log(d2)
                )

    def split_candidates():
        for b in range(ROW):
            ids = jnp.broadcast_to(cbuf[b, 0:1, :], (BLOCK, BLOCK))
            place = lax.broadcasted_iota(jnp.int32, (BLOCK, BLOCK), 0).astype(jnp.float32)
            hit = jnp.max(jnp.where(ids == place, 1.0, 0.0), axis=1, keepdims=True)
            is_cand = jnp.broadcast_to(hit, (BLOCK, BLOCK)) > 0.5
            where = (z * 4 + b // 2, slice(b * BLOCK, (b + 1) * BLOCK), slice((b % 2) * 128, (b % 2) * 128 + 128))
            level = loss[where]
            cand_loss[b] = jnp.where(is_cand, level, NOTHING)
            loss[where] = jnp.where(is_cand, NOTHING, level)

    def turn(source, block, p, row):
        half, first, count = PIECES[p]
        values = source[block, first : first + count, half * 16 : half * 16 + 16, :].astype(jnp.float32)
        turned = jnp.transpose(values, (1, 0, 2)).astype(jnp.bfloat16)
        for t in range(16):
            mixed_in[
                half * 8 + t // 2,
                row * BLOCK + first : row * BLOCK + first + count,
                (t % 2) * 128 : (t % 2) * 128 + 128,
            ] = turned[t]

    def mix(half, b):
        w = wbuf[b % 2, b // 2]

        @pl.loop(0, 8, unroll=8)
        def _(step):
            pair = half * 8 + step
            fresh = mixed_in[pair, b * BLOCK : (b + 4) * BLOCK, :]
            mixed = jnp.dot(w, fresh, preferred_element_type=jnp.float32)
            power = jnp.exp2(loss[pair, b * BLOCK : (b + 1) * BLOCK, :] + FIELD_GAIN * mixed)
            added = jnp.sum(power.reshape(BLOCK // 8, 8, 256), axis=0)
            acc[2 * pair, 0] += added[:, :128]
            acc[2 * pair + 1, 0] += added[:, 128:]

    acc[...] = jnp.zeros_like(acc)

    @pl.when(z == 0)
    def _():
        mixed_in[:, 0 : HALO * BLOCK, :] = jnp.zeros((16, HALO * BLOCK, 256), jnp.bfloat16)

    def halo_in(p):
        @pl.when(z > 0)
        def _():
            for h in range(HALO):
                forward(h, p).wait_recv()
                turn(halo, h, p, h)

    first_half = [p for p in range(PARTS) if PIECES[p][0] == 0]
    second_half = [p for p in range(PARTS) if PIECES[p][0] == 1]
    loss_blocks = {p: [b for b in range(ROW) if b * 3 // ROW == p] for p in range(3)}

    def serve(blocks):
        for b in blocks:
            tile = z * 8 + b
            lanes = slice((b % 2) * 128, (b % 2) * 128 + 128)
            fresh = mixed_in[z * 4 + b // 2, b * BLOCK : (b + 4) * BLOCK, lanes]
            mixed = jnp.dot(wbuf[b % 2, b // 2], fresh, preferred_element_type=jnp.float32)
            level = cand_loss[b]
            power = jnp.exp2(level + FIELD_GAIN * mixed)
            best = jnp.max(power, axis=0, keepdims=True)
            serves = (power == best) & (level > 0.5 * NOTHING)
            ties = jnp.sum(jnp.where(serves, 1.0, 0.0), axis=0, keepdims=True)
            rest = jnp.sum(jnp.where(serves, 0.0, power), axis=0, keepdims=True)
            acc[tile, 0, 0:1, :] += rest + jnp.where(ties > 1.5, (ties - 1.0) * best, 0.0)
            acc[tile, 1, 0:1, :] = best

    def o_copy(to_z, q):
        owner = to_z * 8 + (at_row(*PEERS[q]) if q < 7 else j)
        return remote(
            acc.at[owner], rows.at[z, j], o_send.at[to_z * 8 + q], o_recv.at[z * 8 + j], owner, band
        )

    def hand_over(half):
        for q in range(8):
            for to_z in (2 * half, 2 * half + 1):
                if q < 7:
                    o_copy(to_z, q).start()
                else:
                    @pl.when(to_z != z)
                    def _():
                        o_copy(to_z, q).start()

    def sent(p):
        for q in range(7):
            send(q, p).wait_send()

    def forwarded(pieces):
        @pl.when(z < 3)
        def _():
            for p in pieces:
                for h in range(HALO):
                    forward(h, p).wait_send()

    for p in range(PARTS):
        for h in (1, 2, 0):
            arrived(ROW - HALO + h, p)

            @pl.when(z < 3)
            def _():
                forward(h, p).start()

        if HELD and p == PARTS - HELD - 1:
            @pl.when(j < ROW - HALO)
            def _():
                for k in range(PARTS - HELD, PARTS):
                    for q in range(7):
                        send(q, k).start()

        for b in loss_blocks.get(p, ()):
            path_loss(b)
        if p == 0:
            for dx in (1, 2, 3):
                other = (x + dx) % 4
                got = wbuf.at[c, other, quarter]
                pltpu.make_async_copy(got, got, w_recv.at[other]).wait()
            for dc in (0, 1):
                for dy in range(4):
                    if dc or dy:
                        w2_copy(dc, dy).start()
        if p == 1:
            for q in range(7):
                other = at_row(*PEERS[q])
                pltpu.make_async_copy(cbuf.at[other], cbuf.at[other], c_recv.at[other]).wait()
            for dc in (0, 1):
                for dy in range(4):
                    if dc or dy:
                        other_c, other_y = (c + dc) % 2, (band + dy) % 4
                        got = wbuf.at[other_c, :, pl.ds(pl.multiple_of(other_y * 32, 32), 32)]
                        pltpu.make_async_copy(got, got, w2_recv.at[other_c * 4 + other_y]).wait()
        if p == 2:
            split_candidates()
        for b in range(ROW):
            if b < ROW - HALO:
                arrived(b, p)
            turn(land, b, p, b + HALO)
        if p == first_half[-1]:
            for b in range(HALO, ROW):
                mix(0, b)
        if p == second_half[1]:
            for k in first_half:
                halo_in(k)
            for b in range(HALO):
                mix(0, b)

            @pl.when(z < 2)
            def _():
                serve(range(ROW))

            hand_over(0)
        if p >= 2:
            sent(p - 2)
    for k in second_half[:-1]:
        halo_in(k)
    for b in range(HALO, ROW):
        mix(1, b)

    @pl.when(z >= 2)
    def _():
        serve(range(HALO, ROW))

    sent(PARTS - 2)
    sent(PARTS - 1)
    forwarded(range(PARTS - 1))
    halo_in(second_half[-1])
    for b in range(HALO):
        mix(1, b)

    @pl.when(z >= 2)
    def _():
        serve(range(HALO))

    hand_over(1)
    rows[z, j] = acc[site]
    for dz in range(4):
        for q in range(8 if dz else 7):
            from_z = (z + dz) % 4
            from_j = at_row(*PEERS[q]) if q < 7 else j
            came = rows.at[from_z, from_j]
            pltpu.make_async_copy(came, came, o_recv.at[from_z * 8 + from_j]).wait()
    others = jnp.sum((rows[0, :, 0] + rows[1, :, 0]) + (rows[2, :, 0] + rows[3, :, 0]), axis=1)
    best = jnp.max(rows[z, :, 1], axis=1)
    to_log10 = 1.0 / math.log(10.0)
    best_level = jnp.log(best) * to_log10
    sinr_level = jnp.log(best / others) * to_log10
    total = jnp.sum(sinr_level, axis=0, keepdims=True)
    msum[...] = jnp.broadcast_to(total, (8, 128))

    def m_copy(dy):
        return remote(msum, means.at[band], m_send.at[dy], m_recv.at[band], site, (band + dy) % 4)

    for dy in (1, 2, 3):
        m_copy(dy).start()
    means[band] = msum[...]
    out[0:8, :] = best_level
    out[8:16, :] = sinr_level
    for dy in (1, 2, 3):
        came = (band + dy) % 4
        pltpu.make_async_copy(means.at[came], means.at[came], m_recv.at[came]).wait()
    total = (means[0] + means[1]) + (means[2] + means[3])
    mean = jnp.sum(total, axis=1, keepdims=True) * (1.0 / 4096.0)
    out[16:24, :] = jnp.broadcast_to(mean, (8, 128))

    forwarded(range(PARTS - 1, PARTS))
    for q in range(7):
        c_copy(q).wait_send()
    for to_z in range(4):
        for q in range(7):
            o_copy(to_z, q).wait_send()

        @pl.when(to_z != z)
        def _():
            o_copy(to_z, 7).wait_send()

    for dx in (1, 2, 3):
        w_copy(dx).wait_send()
        m_copy(dx).wait_send()
    for dc in (0, 1):
        for dy in range(4):
            if dc or dy:
                w2_copy(dc, dy).wait_send()


def hand_out(out, best, sinr, mean):
    for k in range(8):
        best[:, k * 128 : (k + 1) * 128] = out[k : k + 1, :]
        sinr[:, k * 128 : (k + 1) * 128] = out[8 + k : 9 + k, :]
    mean[...] = out[16:17, :]


def shards(fields, factor, pattern, tx_power, site_position, candidates):
    dma = pltpu.SemaphoreType.DMA
    f32, bf16 = jnp.float32, jnp.bfloat16
    vmem = pl.BlockSpec(memory_space=pltpu.VMEM)
    out = pl.pallas_call(
        kernel,
        out_shape=jax.ShapeDtypeStruct((24, 128), f32),
        in_specs=[pl.BlockSpec(memory_space=pl.ANY)] * 6,
        out_specs=vmem,
        scratch_shapes=[
            pltpu.VMEM((32, 4, BLOCK), bf16),
            pltpu.VMEM((1, 3), jnp.int32),
            pltpu.VMEM((1, 1024), f32),
            pltpu.VMEM((2, 1024), f32),
            pltpu.VMEM((1, 16), jnp.int32),
            pltpu.VMEM((ROW, BLOCK, 32, 128), bf16),
            pltpu.VMEM((HALO, BLOCK, 32, 128), bf16),
            pltpu.VMEM((16, (HALO + ROW) * BLOCK, 256), bf16),
            pltpu.VMEM((16, ROW * BLOCK, 256), f32),
            pltpu.VMEM((ROW, BLOCK, 128), f32),
            pltpu.VMEM((2, 4, BLOCK, 512), bf16),
            pltpu.VMEM((ROW, BLOCK, 128), f32),
            pltpu.VMEM((ROW, BLOCK, 128), f32),
            pltpu.VMEM((ROW, BLOCK, 128), f32),
            pltpu.VMEM((ROW, 8, 128), f32),
            pltpu.VMEM((32, 2, 8, 128), f32),
            pltpu.VMEM((4, ROW, 2, 8, 128), f32),
            pltpu.VMEM((8, 128), f32),
            pltpu.VMEM((4, 8, 128), f32),
            dma((7 * PARTS,)), dma((8 * PARTS,)), dma((HALO * PARTS,)), dma((HALO * PARTS,)),
            dma((4,)), dma((4,)), dma((8,)), dma((8,)), dma((7,)), dma((8,)),
            dma((32,)), dma((32,)), dma((4,)), dma((4,)), dma((5,)),
        ],
        compiler_params=pltpu.CompilerParams(
            collective_id=0, has_side_effects=True, vmem_limit_bytes=56 << 20
        ),
    )(fields, factor, pattern, tx_power.reshape(1, -1), site_position, candidates)
    best, sinr, mean = pl.pallas_call(
        hand_out,
        out_shape=(
            jax.ShapeDtypeStruct((1, 1024), f32),
            jax.ShapeDtypeStruct((1, 1024), f32),
            jax.ShapeDtypeStruct((1, 128), f32),
        ),
        in_specs=[vmem],
        out_specs=(vmem, vmem, vmem),
    )(out)
    return (best, sinr, mean[0, 0:1])


def solution(mesh):
    placed = (
        P("site", None, "band"),
        P("site", None, None),
        P("site", None),
        P(),
        P(),
        P("site", None),
    )
    return jax.shard_map(
        shards,
        mesh=mesh,
        in_specs=placed,
        out_specs=(P("site", "band"), P("site", "band"), P("site")),
        check_vma=False,
    )
```

```python
import functools
import math

import jax
import jax.numpy as jnp
from jax import lax
from jax.experimental import pallas as pl
from jax.experimental.pallas import tpu as pltpu
from jax.sharding import PartitionSpec as P

MESH = pl.DeviceIdType.MESH
COLS = 256
SPACING = 0.03
PIECES = ((0, 0, 32), (0, 32, 32), (0, 64, 64), (1, 0, 32), (1, 32, 32), (1, 64, 32), (1, 96, 16), (1, 112, 8), (1, 120, 8))
PARTS = len(PIECES)
HELD = 3
HELD_TO = (0, 1, 2, 3, 4, 5, 6)
TRIGGER = PARTS - HELD - 1
BLOCK = 128
HALO = 3
ROW = 8
DB = math.log2(10.0) / 10.0
FIELD_GAIN = 8.0 * DB
NOTHING = -1e30
PEERS = ((0, 1), (1, 0), (3, 0), (1, 1), (3, 1), (2, 0), (2, 1))


def kernel(
    fields, factor, pattern, tx_power, site_position, candidates,
    out,
    factor_in, pattern_in, tx, pos, cand_in,
    land, halo, mixed_in, loss, cand_loss, wbuf, site_x, site_y, site_a, cbuf,
    acc, rows, msum, means,
    send_sem, recv_sem, zs, zr, w_send, w_recv, w2_send, w2_recv, c_send, c_recv,
    o_send, o_recv, m_send, m_recv, local,
):
    site = lax.axis_index("site")
    band = lax.axis_index("band")
    z = site // 8
    j = site % 8
    x = j // 2
    c = j % 2
    quarter = pl.ds(pl.multiple_of(band * 32, 32), 32)
    row_sites = pl.ds(pl.multiple_of(z * 1024, 1024), 1024)
    small = [
        pltpu.make_async_copy(factor.at[quarter], factor_in, local.at[0]),
        pltpu.make_async_copy(pattern, pattern_in, local.at[1]),
        pltpu.make_async_copy(tx_power.at[:, row_sites], tx, local.at[2]),
        pltpu.make_async_copy(site_position.at[:, row_sites], pos, local.at[3]),
        pltpu.make_async_copy(candidates, cand_in, local.at[4]),
    ]
    for copy in small:
        copy.start()

    def at_row(dx, dc):
        return ((x + dx) % 4) * 2 + (c + dc) % 2

    barrier = pltpu.get_barrier_semaphore()
    count = 0
    for dz in range(4):
        for dx, dc in PEERS + (((0, 0),) if dz else ()):
            to = ((z + dz) % 4) * 8 + at_row(dx, dc)
            pl.semaphore_signal(barrier, inc=1, device_id=(to, band), device_id_type=MESH)
            count += 1
    for dy in (1, 2, 3):
        for dc in (0, 1):
            pl.semaphore_signal(
                barrier, inc=1, device_id=(z * 8 + at_row(0, dc), (band + dy) % 4), device_id_type=MESH
            )
            count += 1
    pl.semaphore_wait(barrier, count)

    def remote(src, dst, send, recv, to_site, to_band):
        return pltpu.make_async_remote_copy(
            src_ref=src, dst_ref=dst, send_sem=send, recv_sem=recv,
            device_id=(to_site, to_band), device_id_type=MESH,
        )

    def w_copy(dx):
        mine = wbuf.at[c, x, quarter]
        return remote(mine, mine, w_send.at[dx], w_recv.at[x], z * 8 + at_row(dx, 0), band)

    def w2_copy(dc, dy):
        mine = wbuf.at[c, :, quarter]
        return remote(
            mine, mine, w2_send.at[dc * 4 + dy], w2_recv.at[c * 4 + band],
            z * 8 + at_row(0, dc), (band + dy) % 4,
        )

    def c_copy(q):
        dx, dc = PEERS[q]
        return remote(cbuf.at[j], cbuf.at[j], c_send.at[q], c_recv.at[j], z * 8 + at_row(dx, dc), band)

    def piece(p):
        half, first, count = PIECES[p]
        return pl.ds(first, count), pl.ds(half * 16, 16)

    def chunk(owner, p):
        sites, tiles = piece(p)
        return fields.at[sites, tiles, pl.ds(pl.multiple_of(owner * 128, 128), 128)]

    def landed(block, p):
        sites, tiles = piece(p)
        return land.at[block, sites, tiles]

    def send(q, p):
        dx, dc = PEERS[q]
        owner = at_row(dx, dc)
        return remote(
            chunk(owner, p), landed(j, p), send_sem.at[p], recv_sem.at[j * PARTS + p],
            z * 8 + owner, band,
        )

    def forward(h, p):
        sites, tiles = piece(p)
        return remote(
            landed(ROW - HALO + h, p), halo.at[h, sites, tiles], zs.at[h * PARTS + p], zr.at[h * PARTS + p],
            ((z + 1) % 4) * 8 + j, band,
        )

    for p in range(PARTS):
        pltpu.make_async_copy(chunk(j, p), landed(j, p), recv_sem.at[j * PARTS + p]).start()
    for q in range(7):
        send(q, 0).start()
    for copy in small:
        copy.wait()
    site_row = lax.broadcasted_iota(jnp.int32, (32, BLOCK), 0) + band * 32
    site_column = lax.broadcasted_iota(jnp.int32, (32, BLOCK), 1)
    for d in range(4):
        rows_of = factor_in[:, d, :].astype(jnp.float32)
        if d == 0:
            kept = jnp.where(site_column <= site_row, rows_of, 0.0)
        else:
            present = pattern_in[0:1, d - 1 : d].astype(jnp.float32)
            kept = rows_of * jnp.broadcast_to(present, (32, BLOCK))
        wbuf[c, x, quarter, (3 - d) * BLOCK : (4 - d) * BLOCK] = kept.astype(jnp.bfloat16)
    cbuf[j] = jnp.full((8, 128), -1.0, jnp.float32)
    cbuf[j, 0:1, 0:16] = (cand_in[...] - site * BLOCK).astype(jnp.float32)
    for dx in (1, 2, 3):
        w_copy(dx).start()
    for q in range(7):
        c_copy(q).start()
    for p in range(1, PARTS - HELD):
        for q in range(7):
            send(q, p).start()
    if HELD:
        for p in range(PARTS - HELD, PARTS):
            for q in range(7):
                if q not in HELD_TO:
                    send(q, p).start()

        @pl.when(j >= ROW - HALO)
        def _():
            for p in range(PARTS - HELD, PARTS):
                for q in HELD_TO:
                    send(q, p).start()

    def arrived(block, p):
        ref = landed(block, p)
        pltpu.make_async_copy(ref, ref, recv_sem.at[block * PARTS + p]).wait()

    eight = pl.ds(pl.multiple_of(z * 8, 8), 8)
    for b in range(ROW):
        block = slice(b * BLOCK, (b + 1) * BLOCK)
        xs = pos[0:1, block] * (8.0 * COLS * SPACING)
        ys = pos[1:2, block] * (4.0 * COLS * SPACING)
        level = (tx[0:1, block] - 10.0) * DB
        for ref, values in ((site_x, xs), (site_y, ys), (site_a, level)):
            ref[b] = jnp.transpose(jnp.broadcast_to(values, (BLOCK, BLOCK)))

    lane = lax.broadcasted_iota(jnp.int32, (1, 128), 1)
    column = (j % 2) * 128 + lane
    pixel_row = band * 4 + j // 2

    def path_loss(b):
        @pl.loop(0, 16)
        def _(pair):
            for u in range(2):
                tile = pair * 2 + u
                px = ((tile % 8) * COLS + column).astype(jnp.float32) * SPACING
                py = ((tile // 8) * COLS + pixel_row).astype(jnp.float32) * SPACING
                dx = site_x[b] - px
                dy = site_y[b] - py
                d2 = dx * dx + dy * dy + SPACING * SPACING
                loss[pair, b * BLOCK : (b + 1) * BLOCK, u * 128 : (u + 1) * 128] = (
                    site_a[b] - (1.1 / math.log(2.0)) * jnp.log(d2)
                )

    def split_candidates():
        for b in range(ROW):
            ids = jnp.broadcast_to(cbuf[b, 0:1, :], (BLOCK, BLOCK))
            place = lax.broadcasted_iota(jnp.int32, (BLOCK, BLOCK), 0).astype(jnp.float32)
            hit = jnp.max(jnp.where(ids == place, 1.0, 0.0), axis=1, keepdims=True)
            is_cand = jnp.broadcast_to(hit, (BLOCK, BLOCK)) > 0.5
            where = (z * 4 + b // 2, slice(b * BLOCK, (b + 1) * BLOCK), slice((b % 2) * 128, (b % 2) * 128 + 128))
            level = loss[where]
            cand_loss[b] = jnp.where(is_cand, level, NOTHING)
            loss[where] = jnp.where(is_cand, NOTHING, level)

    def turn(source, block, p, row):
        half, first, count = PIECES[p]
        if count == 8:
            if first % 16 == 0:
                return
            first, count = first - 8, 16
        values = source[block, first : first + count, half * 16 : half * 16 + 16, :].astype(jnp.float32)
        turned = jnp.transpose(values, (1, 0, 2)).astype(jnp.bfloat16)
        for t in range(16):
            mixed_in[
                half * 8 + t // 2,
                row * BLOCK + first : row * BLOCK + first + count,
                (t % 2) * 128 : (t % 2) * 128 + 128,
            ] = turned[t]

    def mix(half, b):
        w = wbuf[b % 2, b // 2]

        @pl.loop(0, 8, unroll=8)
        def _(step):
            pair = half * 8 + step
            fresh = mixed_in[pair, b * BLOCK : (b + 4) * BLOCK, :]
            mixed = jnp.dot(w, fresh, preferred_element_type=jnp.float32)
            power = jnp.exp2(loss[pair, b * BLOCK : (b + 1) * BLOCK, :] + FIELD_GAIN * mixed)
            added = jnp.sum(power.reshape(BLOCK // 8, 8, 256), axis=0)
            acc[2 * pair, 0] += added[:, :128]
            acc[2 * pair + 1, 0] += added[:, 128:]

    acc[...] = jnp.zeros_like(acc)

    @pl.when(z == 0)
    def _():
        mixed_in[:, 0 : HALO * BLOCK, :] = jnp.zeros((16, HALO * BLOCK, 256), jnp.bfloat16)

    def halo_in(p):
        @pl.when(z > 0)
        def _():
            for h in range(HALO):
                forward(h, p).wait_recv()
                turn(halo, h, p, h)

    first_half = [p for p in range(PARTS) if PIECES[p][0] == 0]
    second_half = [p for p in range(PARTS) if PIECES[p][0] == 1]
    loss_blocks = {p: [b for b in range(ROW) if b * 3 // ROW == p] for p in range(3)}

    def serve(blocks):
        for b in blocks:
            tile = z * 8 + b
            lanes = slice((b % 2) * 128, (b % 2) * 128 + 128)
            fresh = mixed_in[z * 4 + b // 2, b * BLOCK : (b + 4) * BLOCK, lanes]
            mixed = jnp.dot(wbuf[b % 2, b // 2], fresh, preferred_element_type=jnp.float32)
            level = cand_loss[b]
            power = jnp.exp2(level + FIELD_GAIN * mixed)
            best = jnp.max(power, axis=0, keepdims=True)
            serves = (power == best) & (level > 0.5 * NOTHING)
            ties = jnp.sum(jnp.where(serves, 1.0, 0.0), axis=0, keepdims=True)
            rest = jnp.sum(jnp.where(serves, 0.0, power), axis=0, keepdims=True)
            acc[tile, 0, 0:1, :] += rest + jnp.where(ties > 1.5, (ties - 1.0) * best, 0.0)
            acc[tile, 1, 0:1, :] = best

    def o_copy(to_z, q):
        owner = to_z * 8 + (at_row(*PEERS[q]) if q < 7 else j)
        return remote(
            acc.at[owner], rows.at[z, j], o_send.at[0], o_recv.at[0], owner, band
        )

    def hand_over(half):
        for q in range(8):
            for to_z in (2 * half, 2 * half + 1):
                if q < 7:
                    o_copy(to_z, q).start()
                else:
                    @pl.when(to_z != z)
                    def _():
                        o_copy(to_z, q).start()

    def sent(p):
        sites, tiles = piece(p)
        seven = land.at[pl.ds(0, 7), sites, tiles]
        pltpu.make_async_copy(seven, seven, send_sem.at[p]).wait()

    def forwarded(pieces):
        @pl.when(z < 3)
        def _():
            for p in pieces:
                for h in range(HALO):
                    forward(h, p).wait_send()

    def pass_on(p):
        for h in (1, 2, 0):
            arrived(ROW - HALO + h, p)

            @pl.when(z < 3)
            def _():
                forward(h, p).start()

        if HELD and p == TRIGGER:
            @pl.when(j < ROW - HALO)
            def _():
                for k in range(PARTS - HELD, PARTS):
                    for q in HELD_TO:
                        send(q, k).start()

    for p in range(PARTS - HELD):
        pass_on(p)
        for b in loss_blocks.get(p, ()):
            path_loss(b)
        if p == 0:
            for dx in (1, 2, 3):
                other = (x + dx) % 4
                got = wbuf.at[c, other, quarter]
                pltpu.make_async_copy(got, got, w_recv.at[other]).wait()
            for dc in (0, 1):
                for dy in range(4):
                    if dc or dy:
                        w2_copy(dc, dy).start()
        if p == 1:
            for q in range(7):
                other = at_row(*PEERS[q])
                pltpu.make_async_copy(cbuf.at[other], cbuf.at[other], c_recv.at[other]).wait()
            for dc in (0, 1):
                for dy in range(4):
                    if dc or dy:
                        other_c, other_y = (c + dc) % 2, (band + dy) % 4
                        got = wbuf.at[other_c, :, pl.ds(pl.multiple_of(other_y * 32, 32), 32)]
                        pltpu.make_async_copy(got, got, w2_recv.at[other_c * 4 + other_y]).wait()
        if p == 2:
            split_candidates()
        for b in range(ROW):
            if b < ROW - HALO:
                arrived(b, p)
            turn(land, b, p, b + HALO)
        if p == first_half[-1]:
            for b in range(HALO, ROW):
                mix(0, b)
        if p == second_half[1]:
            for k in first_half:
                halo_in(k)
            for b in range(HALO):
                mix(0, b)

            @pl.when(z < 2)
            def _():
                serve(range(ROW))

            hand_over(0)
        if p == 3:
            for q in range(7):
                c_copy(q).wait_send()
            for dx in (1, 2, 3):
                w_copy(dx).wait_send()
            for dc in (0, 1):
                for dy in range(4):
                    if dc or dy:
                        w2_copy(dc, dy).wait_send()
        if p >= 2:
            sent(p - 2)
    held = range(PARTS - HELD, PARTS)
    for p in held:
        pass_on(p)
        for b in range(ROW - HALO, ROW):
            turn(land, b, p, b + HALO)
    late = held if HELD else (PARTS - 2, PARTS - 1)
    for k in second_half:
        if k not in late:
            halo_in(k)
    for p in range(PARTS - HELD - 2, PARTS - HELD):
        sent(p)
    forwarded(range(PARTS - HELD))
    for p in held:
        for b in range(ROW - HALO):
            arrived(b, p)
            turn(land, b, p, b + HALO)
    for b in range(HALO, ROW):
        mix(1, b)

    @pl.when(z >= 2)
    def _():
        serve(range(HALO, ROW))

    for p in held:
        sent(p)
    forwarded(held)
    for p in late:
        halo_in(p)
    for b in range(HALO):
        mix(1, b)

    @pl.when(z >= 2)
    def _():
        serve(range(HALO))

    hand_over(1)
    pltpu.make_async_copy(acc.at[site], rows.at[z, j], o_recv.at[0]).start()
    pltpu.make_async_copy(rows, rows, o_recv.at[0]).wait()
    others = jnp.sum((rows[0, :, 0] + rows[1, :, 0]) + (rows[2, :, 0] + rows[3, :, 0]), axis=1)
    best = jnp.max(rows[z, :, 1], axis=1)
    to_log10 = 1.0 / math.log(10.0)
    best_level = jnp.log(best) * to_log10
    sinr_level = jnp.log(best / others) * to_log10
    total = jnp.sum(sinr_level, axis=0, keepdims=True)
    msum[...] = jnp.broadcast_to(total, (8, 128))

    def m_copy(dy):
        return remote(msum, means.at[band], m_send.at[dy], m_recv.at[band], site, (band + dy) % 4)

    for dy in (1, 2, 3):
        m_copy(dy).start()
    means[band] = msum[...]
    out[0:8, :] = best_level
    out[8:16, :] = sinr_level
    for dy in (1, 2, 3):
        came = (band + dy) % 4
        pltpu.make_async_copy(means.at[came], means.at[came], m_recv.at[came]).wait()
    total = (means[0] + means[1]) + (means[2] + means[3])
    mean = jnp.sum(total, axis=1, keepdims=True) * (1.0 / 4096.0)
    out[16:24, :] = jnp.broadcast_to(mean, (8, 128))

    handed = acc.at[pl.ds(0, 31)]
    pltpu.make_async_copy(handed, handed, o_send.at[0]).wait()
    for dx in (1, 2, 3):
        m_copy(dx).wait_send()


def hand_out(out, best, sinr, mean):
    for k in range(8):
        best[:, k * 128 : (k + 1) * 128] = out[k : k + 1, :]
        sinr[:, k * 128 : (k + 1) * 128] = out[8 + k : 9 + k, :]
    mean[...] = out[16:17, :]


def shards(fields, factor, pattern, tx_power, site_position, candidates):
    dma = pltpu.SemaphoreType.DMA
    f32, bf16 = jnp.float32, jnp.bfloat16
    vmem = pl.BlockSpec(memory_space=pltpu.VMEM)
    out = pl.pallas_call(
        kernel,
        out_shape=pltpu.VMEM((24, 128), f32),
        in_specs=[pl.BlockSpec(memory_space=pl.ANY)] * 6,
        out_specs=vmem,
        scratch_shapes=[
            pltpu.VMEM((32, 4, BLOCK), bf16),
            pltpu.VMEM((1, 3), jnp.int32),
            pltpu.VMEM((1, 1024), f32),
            pltpu.VMEM((2, 1024), f32),
            pltpu.VMEM((1, 16), jnp.int32),
            pltpu.VMEM((ROW, BLOCK, 32, 128), bf16),
            pltpu.VMEM((HALO, BLOCK, 32, 128), bf16),
            pltpu.VMEM((16, (HALO + ROW) * BLOCK, 256), bf16),
            pltpu.VMEM((16, ROW * BLOCK, 256), f32),
            pltpu.VMEM((ROW, BLOCK, 128), f32),
            pltpu.VMEM((2, 4, BLOCK, 512), bf16),
            pltpu.VMEM((ROW, BLOCK, 128), f32),
            pltpu.VMEM((ROW, BLOCK, 128), f32),
            pltpu.VMEM((ROW, BLOCK, 128), f32),
            pltpu.VMEM((ROW, 8, 128), f32),
            pltpu.VMEM((32, 2, 8, 128), f32),
            pltpu.VMEM((4, ROW, 2, 8, 128), f32),
            pltpu.VMEM((8, 128), f32),
            pltpu.VMEM((4, 8, 128), f32),
            dma((PARTS,)), dma((8 * PARTS,)), dma((HALO * PARTS,)), dma((HALO * PARTS,)),
            dma((4,)), dma((4,)), dma((8,)), dma((8,)), dma((7,)), dma((8,)),
            dma((1,)), dma((1,)), dma((4,)), dma((4,)), dma((5,)),
        ],
        compiler_params=pltpu.CompilerParams(
            collective_id=0, has_side_effects=True, vmem_limit_bytes=56 << 20
        ),
    )(fields, factor, pattern, tx_power.reshape(1, -1), site_position, candidates)
    best, sinr, mean = pl.pallas_call(
        hand_out,
        out_shape=(
            jax.ShapeDtypeStruct((1, 1024), f32),
            jax.ShapeDtypeStruct((1, 1024), f32),
            jax.ShapeDtypeStruct((1, 128), f32),
        ),
        in_specs=[vmem],
        out_specs=(vmem, vmem, vmem),
    )(out)
    return (best, sinr, mean[0, 0:1])


def solution(mesh):
    placed = (
        P("site", None, "band"),
        P("site", None, None),
        P("site", None),
        P(),
        P(),
        P("site", None),
    )
    return jax.shard_map(
        shards,
        mesh=mesh,
        in_specs=placed,
        out_specs=(P("site", "band"), P("site", "band"), P("site")),
        check_vma=False,
    )
```

```python
import functools
import math

import jax
import jax.numpy as jnp
from jax import lax
from jax.experimental import pallas as pl
from jax.experimental.pallas import tpu as pltpu
from jax.sharding import PartitionSpec as P

MESH = pl.DeviceIdType.MESH
COLS = 256
SPACING = 0.03
PIECES = ((0, 0, 32), (0, 32, 32), (0, 64, 64), (1, 0, 32), (1, 32, 32), (1, 64, 32), (1, 96, 16), (1, 112, 8), (1, 120, 8))
PARTS = len(PIECES)
HELD = 3
HELD_TO = (0, 1, 2, 3, 4, 5, 6)
TRIGGER = PARTS - HELD - 1
BLOCK = 128
HALO = 3
ROW = 8
DB = math.log2(10.0) / 10.0
FIELD_GAIN = 8.0 * DB
NOTHING = -1e30
PEERS = ((0, 1), (1, 0), (3, 0), (1, 1), (3, 1), (2, 0), (2, 1))


def kernel(
    fields, factor, pattern, tx_power, site_position, candidates,
    out,
    factor_in, pattern_in, tx, pos, cand_in,
    land, halo, mixed_in, loss, cand_loss, wbuf, site_x, site_y, site_a, cbuf,
    acc, rows, msum, means,
    send_sem, recv_sem, zs, zr, w_send, w_recv, w2_send, w2_recv, c_send, c_recv,
    o_send, o_recv, m_send, m_recv, local,
):
    site = lax.axis_index("site")
    band = lax.axis_index("band")
    z = site // 8
    j = site % 8
    x = j // 2
    c = j % 2
    quarter = pl.ds(pl.multiple_of(band * 32, 32), 32)
    row_sites = pl.ds(pl.multiple_of(z * 1024, 1024), 1024)
    small = [
        pltpu.make_async_copy(factor.at[quarter], factor_in, local.at[0]),
        pltpu.make_async_copy(pattern, pattern_in, local.at[1]),
        pltpu.make_async_copy(tx_power.at[:, row_sites], tx, local.at[2]),
        pltpu.make_async_copy(site_position.at[:, row_sites], pos, local.at[3]),
        pltpu.make_async_copy(candidates, cand_in, local.at[4]),
    ]
    for copy in small:
        copy.start()

    def at_row(dx, dc):
        return ((x + dx) % 4) * 2 + (c + dc) % 2

    barrier = pltpu.get_barrier_semaphore()
    count = 0
    for dz in range(4):
        for dx, dc in PEERS + (((0, 0),) if dz else ()):
            to = ((z + dz) % 4) * 8 + at_row(dx, dc)
            pl.semaphore_signal(barrier, inc=1, device_id=(to, band), device_id_type=MESH)
            count += 1
    for dy in (1, 2, 3):
        for dc in (0, 1):
            pl.semaphore_signal(
                barrier, inc=1, device_id=(z * 8 + at_row(0, dc), (band + dy) % 4), device_id_type=MESH
            )
            count += 1
    pl.semaphore_wait(barrier, count)

    def remote(src, dst, send, recv, to_site, to_band):
        return pltpu.make_async_remote_copy(
            src_ref=src, dst_ref=dst, send_sem=send, recv_sem=recv,
            device_id=(to_site, to_band), device_id_type=MESH,
        )

    def w_copy(dx):
        mine = wbuf.at[c, x, quarter]
        return remote(mine, mine, w_send.at[dx], w_recv.at[x], z * 8 + at_row(dx, 0), band)

    def w2_copy(dc, dy):
        mine = wbuf.at[c, :, quarter]
        return remote(
            mine, mine, w2_send.at[dc * 4 + dy], w2_recv.at[c * 4 + band],
            z * 8 + at_row(0, dc), (band + dy) % 4,
        )

    def c_copy(q):
        dx, dc = PEERS[q]
        return remote(cbuf.at[j], cbuf.at[j], c_send.at[q], c_recv.at[j], z * 8 + at_row(dx, dc), band)

    def piece(p):
        half, first, count = PIECES[p]
        return pl.ds(first, count), pl.ds(half * 16, 16)

    def chunk(owner, p):
        sites, tiles = piece(p)
        return fields.at[sites, tiles, pl.ds(pl.multiple_of(owner * 128, 128), 128)]

    def landed(block, p):
        sites, tiles = piece(p)
        return land.at[block, sites, tiles]

    def send(q, p):
        dx, dc = PEERS[q]
        owner = at_row(dx, dc)
        return remote(
            chunk(owner, p), landed(j, p), send_sem.at[p], recv_sem.at[j * PARTS + p],
            z * 8 + owner, band,
        )

    def forward(h, p):
        sites, tiles = piece(p)
        return remote(
            landed(ROW - HALO + h, p), halo.at[h, sites, tiles], zs.at[h * PARTS + p], zr.at[h * PARTS + p],
            ((z + 1) % 4) * 8 + j, band,
        )

    for p in range(PARTS):
        pltpu.make_async_copy(chunk(j, p), landed(j, p), recv_sem.at[j * PARTS + p]).start()
    for q in range(7):
        send(q, 0).start()
    for copy in small:
        copy.wait()
    site_row = lax.broadcasted_iota(jnp.int32, (32, BLOCK), 0) + band * 32
    site_column = lax.broadcasted_iota(jnp.int32, (32, BLOCK), 1)
    for d in range(4):
        rows_of = factor_in[:, d, :].astype(jnp.float32)
        if d == 0:
            kept = jnp.where(site_column <= site_row, rows_of, 0.0)
        else:
            present = pattern_in[0:1, d - 1 : d].astype(jnp.float32)
            kept = rows_of * jnp.broadcast_to(present, (32, BLOCK))
        wbuf[c, x, quarter, (3 - d) * BLOCK : (4 - d) * BLOCK] = kept.astype(jnp.bfloat16)
    cbuf[j] = jnp.full((8, 128), -1.0, jnp.float32)
    cbuf[j, 0:1, 0:16] = (cand_in[...] - site * BLOCK).astype(jnp.float32)
    for dx in (1, 2, 3):
        w_copy(dx).start()
    for q in range(7):
        c_copy(q).start()
    for p in range(1, PARTS - HELD):
        for q in range(7):
            send(q, p).start()
    if HELD:
        for p in range(PARTS - HELD, PARTS):
            for q in range(7):
                if q not in HELD_TO:
                    send(q, p).start()

        @pl.when(j >= ROW - HALO)
        def _():
            for p in range(PARTS - HELD, PARTS):
                for q in HELD_TO:
                    send(q, p).start()

    def arrived(block, p):
        ref = landed(block, p)
        pltpu.make_async_copy(ref, ref, recv_sem.at[block * PARTS + p]).wait()

    eight = pl.ds(pl.multiple_of(z * 8, 8), 8)
    for b in range(ROW):
        block = slice(b * BLOCK, (b + 1) * BLOCK)
        xs = pos[0:1, block] * (8.0 * COLS * SPACING)
        ys = pos[1:2, block] * (4.0 * COLS * SPACING)
        level = (tx[0:1, block] - 10.0) * DB
        for ref, values in ((site_x, xs), (site_y, ys), (site_a, level)):
            ref[b] = jnp.transpose(jnp.broadcast_to(values, (BLOCK, BLOCK)))

    lane = lax.broadcasted_iota(jnp.int32, (1, 128), 1)
    column = (j % 2) * 128 + lane
    pixel_row = band * 4 + j // 2

    def path_loss(b):
        @pl.loop(0, 16)
        def _(pair):
            for u in range(2):
                tile = pair * 2 + u
                px = ((tile % 8) * COLS + column).astype(jnp.float32) * SPACING
                py = ((tile // 8) * COLS + pixel_row).astype(jnp.float32) * SPACING
                dx = site_x[b] - px
                dy = site_y[b] - py
                d2 = dx * dx + dy * dy + SPACING * SPACING
                loss[pair, b * BLOCK : (b + 1) * BLOCK, u * 128 : (u + 1) * 128] = (
                    site_a[b] - (1.1 / math.log(2.0)) * jnp.log(d2)
                )

    def split_candidates():
        for b in range(ROW):
            ids = jnp.broadcast_to(cbuf[b, 0:1, :], (BLOCK, BLOCK))
            place = lax.broadcasted_iota(jnp.int32, (BLOCK, BLOCK), 0).astype(jnp.float32)
            hit = jnp.max(jnp.where(ids == place, 1.0, 0.0), axis=1, keepdims=True)
            is_cand = jnp.broadcast_to(hit, (BLOCK, BLOCK)) > 0.5
            where = (z * 4 + b // 2, slice(b * BLOCK, (b + 1) * BLOCK), slice((b % 2) * 128, (b % 2) * 128 + 128))
            level = loss[where]
            cand_loss[b] = jnp.where(is_cand, level, NOTHING)
            loss[where] = jnp.where(is_cand, NOTHING, level)

    def turn(source, block, p, row):
        half, first, count = PIECES[p]
        if count == 8:
            if first % 16 == 0:
                return
            first, count = first - 8, 16
        values = source[block, first : first + count, half * 16 : half * 16 + 16, :].astype(jnp.float32)
        turned = jnp.transpose(values, (1, 0, 2)).astype(jnp.bfloat16)
        for t in range(16):
            mixed_in[
                half * 8 + t // 2,
                row * BLOCK + first : row * BLOCK + first + count,
                (t % 2) * 128 : (t % 2) * 128 + 128,
            ] = turned[t]

    def mix(half, b):
        w = wbuf[b % 2, b // 2]

        @pl.loop(0, 8, unroll=8)
        def _(step):
            pair = half * 8 + step
            fresh = mixed_in[pair, b * BLOCK : (b + 4) * BLOCK, :]
            mixed = jnp.dot(w, fresh, preferred_element_type=jnp.float32)
            power = jnp.exp2(loss[pair, b * BLOCK : (b + 1) * BLOCK, :] + FIELD_GAIN * mixed)
            added = jnp.sum(power.reshape(BLOCK // 8, 8, 256), axis=0)
            acc[2 * pair, 0] += added[:, :128]
            acc[2 * pair + 1, 0] += added[:, 128:]

    acc[...] = jnp.zeros_like(acc)

    @pl.when(z == 0)
    def _():
        mixed_in[:, 0 : HALO * BLOCK, :] = jnp.zeros((16, HALO * BLOCK, 256), jnp.bfloat16)

    def halo_in(p):
        @pl.when(z > 0)
        def _():
            for h in range(HALO):
                forward(h, p).wait_recv()
                turn(halo, h, p, h)

    first_half = [p for p in range(PARTS) if PIECES[p][0] == 0]
    second_half = [p for p in range(PARTS) if PIECES[p][0] == 1]
    loss_blocks = {p: [b for b in range(ROW) if b * 3 // ROW == p] for p in range(3)}

    def serve(blocks):
        found = []
        for b in blocks:
            lanes = slice((b % 2) * 128, (b % 2) * 128 + 128)
            fresh = mixed_in[z * 4 + b // 2, b * BLOCK : (b + 4) * BLOCK, lanes]
            mixed = jnp.dot(wbuf[b % 2, b // 2], fresh, preferred_element_type=jnp.float32)
            level = cand_loss[b]
            power = jnp.exp2(level + FIELD_GAIN * mixed)
            best = jnp.max(power, axis=0, keepdims=True)
            serves = (power == best) & (level > 0.5 * NOTHING)
            ties = jnp.sum(jnp.where(serves, 1.0, 0.0), axis=0, keepdims=True)
            rest = jnp.sum(jnp.where(serves, 0.0, power), axis=0, keepdims=True)
            found.append((z * 8 + b, best, rest + jnp.where(ties > 1.5, (ties - 1.0) * best, 0.0)))
        for tile, best, rest in found:
            acc[tile, 0, 0:1, :] += rest
            acc[tile, 1, 0:1, :] = best

    def o_copy(to_z, q):
        owner = to_z * 8 + (at_row(*PEERS[q]) if q < 7 else j)
        return remote(
            acc.at[owner], rows.at[z, j], o_send.at[0], o_recv.at[0], owner, band
        )

    def hand_over(half):
        for q in range(8):
            for to_z in (2 * half, 2 * half + 1):
                if q < 7:
                    o_copy(to_z, q).start()
                else:
                    @pl.when(to_z != z)
                    def _():
                        o_copy(to_z, q).start()

    def sent(p):
        sites, tiles = piece(p)
        seven = land.at[pl.ds(0, 7), sites, tiles]
        pltpu.make_async_copy(seven, seven, send_sem.at[p]).wait()

    def forwarded(pieces):
        @pl.when(z < 3)
        def _():
            for p in pieces:
                for h in range(HALO):
                    forward(h, p).wait_send()

    def pass_on(p):
        for h in (1, 2, 0):
            arrived(ROW - HALO + h, p)

            @pl.when(z < 3)
            def _():
                forward(h, p).start()

        if HELD and p == TRIGGER:
            @pl.when(j < ROW - HALO)
            def _():
                for k in range(PARTS - HELD, PARTS):
                    for q in HELD_TO:
                        send(q, k).start()

    for p in range(PARTS - HELD):
        pass_on(p)
        for b in loss_blocks.get(p, ()):
            path_loss(b)
        if p == 0:
            for dx in (1, 2, 3):
                other = (x + dx) % 4
                got = wbuf.at[c, other, quarter]
                pltpu.make_async_copy(got, got, w_recv.at[other]).wait()
            for dc in (0, 1):
                for dy in range(4):
                    if dc or dy:
                        w2_copy(dc, dy).start()
        if p == 1:
            for q in range(7):
                other = at_row(*PEERS[q])
                pltpu.make_async_copy(cbuf.at[other], cbuf.at[other], c_recv.at[other]).wait()
            for dc in (0, 1):
                for dy in range(4):
                    if dc or dy:
                        other_c, other_y = (c + dc) % 2, (band + dy) % 4
                        got = wbuf.at[other_c, :, pl.ds(pl.multiple_of(other_y * 32, 32), 32)]
                        pltpu.make_async_copy(got, got, w2_recv.at[other_c * 4 + other_y]).wait()
        if p == 2:
            split_candidates()
        for b in range(ROW):
            if b < ROW - HALO:
                arrived(b, p)
            turn(land, b, p, b + HALO)
        if p == first_half[-1]:
            for b in range(HALO, ROW):
                mix(0, b)
        if p == second_half[1]:
            for k in first_half:
                halo_in(k)
            for b in range(HALO):
                mix(0, b)

            @pl.when(z < 2)
            def _():
                serve(range(ROW))

            hand_over(0)
        if p == 3:
            for q in range(7):
                c_copy(q).wait_send()
            for dx in (1, 2, 3):
                w_copy(dx).wait_send()
            for dc in (0, 1):
                for dy in range(4):
                    if dc or dy:
                        w2_copy(dc, dy).wait_send()
        if p >= 2:
            sent(p - 2)
    held = range(PARTS - HELD, PARTS)
    for p in held:
        pass_on(p)
        for b in range(ROW - HALO, ROW):
            turn(land, b, p, b + HALO)
    late = held if HELD else (PARTS - 2, PARTS - 1)
    for k in second_half:
        if k not in late:
            halo_in(k)
    for p in range(PARTS - HELD - 2, PARTS - HELD):
        sent(p)
    forwarded(range(PARTS - HELD))
    for p in held:
        for b in range(ROW - HALO):
            arrived(b, p)
            turn(land, b, p, b + HALO)
    for b in range(HALO, ROW):
        mix(1, b)

    @pl.when(z >= 2)
    def _():
        serve(range(HALO, ROW))

    for p in late:
        halo_in(p)
    for b in range(HALO):
        mix(1, b)

    @pl.when(z >= 2)
    def _():
        serve(range(HALO))

    hand_over(1)
    for p in held:
        sent(p)
    forwarded(held)
    pltpu.make_async_copy(acc.at[site], rows.at[z, j], o_recv.at[0]).start()
    pltpu.make_async_copy(rows, rows, o_recv.at[0]).wait()
    others = jnp.sum((rows[0, :, 0] + rows[1, :, 0]) + (rows[2, :, 0] + rows[3, :, 0]), axis=1)
    best = jnp.max(rows[z, :, 1], axis=1)
    to_log10 = 1.0 / math.log(10.0)
    best_level = jnp.log(best) * to_log10
    sinr_level = jnp.log(best / others) * to_log10
    total = jnp.sum(sinr_level, axis=0, keepdims=True)
    msum[...] = jnp.broadcast_to(total, (8, 128))

    def m_copy(dy):
        return remote(msum, means.at[band], m_send.at[dy], m_recv.at[band], site, (band + dy) % 4)

    for dy in (1, 2, 3):
        m_copy(dy).start()
    means[band] = msum[...]
    out[0:8, :] = best_level
    out[8:16, :] = sinr_level
    for dy in (1, 2, 3):
        came = (band + dy) % 4
        pltpu.make_async_copy(means.at[came], means.at[came], m_recv.at[came]).wait()
    total = (means[0] + means[1]) + (means[2] + means[3])
    mean = jnp.sum(total, axis=1, keepdims=True) * (1.0 / 4096.0)
    out[16:24, :] = jnp.broadcast_to(mean, (8, 128))

    handed = acc.at[pl.ds(0, 31)]
    pltpu.make_async_copy(handed, handed, o_send.at[0]).wait()
    for dx in (1, 2, 3):
        m_copy(dx).wait_send()


def hand_out(out, best, sinr, mean):
    for k in range(8):
        best[:, k * 128 : (k + 1) * 128] = out[k : k + 1, :]
        sinr[:, k * 128 : (k + 1) * 128] = out[8 + k : 9 + k, :]
    mean[...] = out[16:17, :]


def shards(fields, factor, pattern, tx_power, site_position, candidates):
    dma = pltpu.SemaphoreType.DMA
    f32, bf16 = jnp.float32, jnp.bfloat16
    vmem = pl.BlockSpec(memory_space=pltpu.VMEM)
    out = pl.pallas_call(
        kernel,
        out_shape=pltpu.VMEM((24, 128), f32),
        in_specs=[pl.BlockSpec(memory_space=pl.ANY)] * 6,
        out_specs=vmem,
        scratch_shapes=[
            pltpu.VMEM((32, 4, BLOCK), bf16),
            pltpu.VMEM((1, 3), jnp.int32),
            pltpu.VMEM((1, 1024), f32),
            pltpu.VMEM((2, 1024), f32),
            pltpu.VMEM((1, 16), jnp.int32),
            pltpu.VMEM((ROW, BLOCK, 32, 128), bf16),
            pltpu.VMEM((HALO, BLOCK, 32, 128), bf16),
            pltpu.VMEM((16, (HALO + ROW) * BLOCK, 256), bf16),
            pltpu.VMEM((16, ROW * BLOCK, 256), f32),
            pltpu.VMEM((ROW, BLOCK, 128), f32),
            pltpu.VMEM((2, 4, BLOCK, 512), bf16),
            pltpu.VMEM((ROW, BLOCK, 128), f32),
            pltpu.VMEM((ROW, BLOCK, 128), f32),
            pltpu.VMEM((ROW, BLOCK, 128), f32),
            pltpu.VMEM((ROW, 8, 128), f32),
            pltpu.VMEM((32, 2, 8, 128), f32),
            pltpu.VMEM((4, ROW, 2, 8, 128), f32),
            pltpu.VMEM((8, 128), f32),
            pltpu.VMEM((4, 8, 128), f32),
            dma((PARTS,)), dma((8 * PARTS,)), dma((HALO * PARTS,)), dma((HALO * PARTS,)),
            dma((4,)), dma((4,)), dma((8,)), dma((8,)), dma((7,)), dma((8,)),
            dma((1,)), dma((1,)), dma((4,)), dma((4,)), dma((5,)),
        ],
        compiler_params=pltpu.CompilerParams(
            collective_id=0, has_side_effects=True, vmem_limit_bytes=56 << 20
        ),
    )(fields, factor, pattern, tx_power.reshape(1, -1), site_position, candidates)
    best, sinr, mean = pl.pallas_call(
        hand_out,
        out_shape=(
            jax.ShapeDtypeStruct((1, 1024), f32),
            jax.ShapeDtypeStruct((1, 1024), f32),
            jax.ShapeDtypeStruct((1, 128), f32),
        ),
        in_specs=[vmem],
        out_specs=(vmem, vmem, vmem),
    )(out)
    return (best, sinr, mean[0, 0:1])


def solution(mesh):
    placed = (
        P("site", None, "band"),
        P("site", None, None),
        P("site", None),
        P(),
        P(),
        P("site", None),
    )
    return jax.shard_map(
        shards,
        mesh=mesh,
        in_specs=placed,
        out_specs=(P("site", "band"), P("site", "band"), P("site")),
        check_vma=False,
    )
```

```python
import functools
import math

import jax
import jax.numpy as jnp
from jax import lax
from jax.experimental import pallas as pl
from jax.experimental.pallas import tpu as pltpu
from jax.sharding import PartitionSpec as P

MESH = pl.DeviceIdType.MESH
COLS = 256
SPACING = 0.03
PIECES = ((0, 0, 32), (0, 32, 32), (0, 64, 64), (1, 0, 32), (1, 32, 32), (1, 64, 32), (1, 96, 16), (1, 112, 8), (1, 120, 8))
PARTS = len(PIECES)
HELD = 3
HELD_TO = (0, 1, 2, 3, 4, 5, 6)
TRIGGER = PARTS - HELD - 1
BLOCK = 128
HALO = 3
ROW = 8
DB = math.log2(10.0) / 10.0
FIELD_GAIN = 8.0 * DB
NOTHING = -1e30
PEERS = ((0, 1), (1, 0), (3, 0), (1, 1), (3, 1), (2, 0), (2, 1))


def kernel(
    fields, factor, pattern, tx_power, site_position, candidates,
    out,
    factor_in, pattern_in, tx, pos, cand_in,
    land, halo, mixed_in, loss, cand_loss, wbuf, site_x, site_y, site_a, cbuf,
    acc, rows, msum, means,
    send_sem, recv_sem, zs, zr, w_send, w_recv, w2_send, w2_recv, c_send, c_recv,
    o_send, o_recv, m_send, m_recv, local,
):
    site = lax.axis_index("site")
    band = lax.axis_index("band")
    z = site // 8
    j = site % 8
    x = j // 2
    c = j % 2
    quarter = pl.ds(pl.multiple_of(band * 32, 32), 32)
    row_sites = pl.ds(pl.multiple_of(z * 1024, 1024), 1024)
    small = [
        pltpu.make_async_copy(factor.at[quarter], factor_in, local.at[0]),
        pltpu.make_async_copy(pattern, pattern_in, local.at[1]),
        pltpu.make_async_copy(tx_power.at[:, row_sites], tx, local.at[2]),
        pltpu.make_async_copy(site_position.at[:, row_sites], pos, local.at[3]),
        pltpu.make_async_copy(candidates, cand_in, local.at[4]),
    ]
    for copy in small:
        copy.start()

    def at_row(dx, dc):
        return ((x + dx) % 4) * 2 + (c + dc) % 2

    barrier = pltpu.get_barrier_semaphore()
    count = 0
    for dz in range(4):
        for dx, dc in PEERS + (((0, 0),) if dz else ()):
            to = ((z + dz) % 4) * 8 + at_row(dx, dc)
            pl.semaphore_signal(barrier, inc=1, device_id=(to, band), device_id_type=MESH)
            count += 1
    for dy in (1, 2, 3):
        for dc in (0, 1):
            pl.semaphore_signal(
                barrier, inc=1, device_id=(z * 8 + at_row(0, dc), (band + dy) % 4), device_id_type=MESH
            )
            count += 1
    pl.semaphore_wait(barrier, count)

    def remote(src, dst, send, recv, to_site, to_band):
        return pltpu.make_async_remote_copy(
            src_ref=src, dst_ref=dst, send_sem=send, recv_sem=recv,
            device_id=(to_site, to_band), device_id_type=MESH,
        )

    def w_copy(dx):
        mine = wbuf.at[c, x, quarter]
        return remote(mine, mine, w_send.at[dx], w_recv.at[x], z * 8 + at_row(dx, 0), band)

    def w2_copy(dc, dy):
        mine = wbuf.at[c, :, quarter]
        return remote(
            mine, mine, w2_send.at[dc * 4 + dy], w2_recv.at[c * 4 + band],
            z * 8 + at_row(0, dc), (band + dy) % 4,
        )

    def c_copy(q):
        dx, dc = PEERS[q]
        return remote(cbuf.at[j], cbuf.at[j], c_send.at[q], c_recv.at[j], z * 8 + at_row(dx, dc), band)

    def piece(p):
        half, first, count = PIECES[p]
        return pl.ds(first, count), pl.ds(half * 16, 16)

    def chunk(owner, p):
        sites, tiles = piece(p)
        return fields.at[sites, tiles, pl.ds(pl.multiple_of(owner * 128, 128), 128)]

    def landed(block, p):
        sites, tiles = piece(p)
        return land.at[block, sites, tiles]

    def send(q, p):
        dx, dc = PEERS[q]
        owner = at_row(dx, dc)
        return remote(
            chunk(owner, p), landed(j, p), send_sem.at[p], recv_sem.at[j * PARTS + p],
            z * 8 + owner, band,
        )

    def forward(h, p):
        sites, tiles = piece(p)
        return remote(
            landed(ROW - HALO + h, p), halo.at[h, sites, tiles], zs.at[h * PARTS + p], zr.at[h * PARTS + p],
            ((z + 1) % 4) * 8 + j, band,
        )

    for p in range(PARTS):
        pltpu.make_async_copy(chunk(j, p), landed(j, p), recv_sem.at[j * PARTS + p]).start()
    for q in range(7):
        send(q, 0).start()
    for copy in small:
        copy.wait()
    site_row = lax.broadcasted_iota(jnp.int32, (32, BLOCK), 0) + band * 32
    site_column = lax.broadcasted_iota(jnp.int32, (32, BLOCK), 1)
    for d in range(4):
        rows_of = factor_in[:, d, :].astype(jnp.float32)
        if d == 0:
            kept = jnp.where(site_column <= site_row, rows_of, 0.0)
        else:
            present = pattern_in[0:1, d - 1 : d].astype(jnp.float32)
            kept = rows_of * jnp.broadcast_to(present, (32, BLOCK))
        wbuf[c, x, quarter, (3 - d) * BLOCK : (4 - d) * BLOCK] = kept.astype(jnp.bfloat16)
    cbuf[j] = jnp.full((8, 128), -1.0, jnp.float32)
    cbuf[j, 0:1, 0:16] = (cand_in[...] - site * BLOCK).astype(jnp.float32)
    for dx in (1, 2, 3):
        w_copy(dx).start()
    for q in range(7):
        c_copy(q).start()
    for p in range(1, PARTS - HELD):
        for q in range(7):
            send(q, p).start()
    if HELD:
        for p in range(PARTS - HELD, PARTS):
            for q in range(7):
                if q not in HELD_TO:
                    send(q, p).start()

        @pl.when(j >= 4)
        def _():
            for p in range(PARTS - HELD, PARTS):
                for q in HELD_TO:
                    send(q, p).start()

    def arrived(block, p):
        ref = landed(block, p)
        pltpu.make_async_copy(ref, ref, recv_sem.at[block * PARTS + p]).wait()

    eight = pl.ds(pl.multiple_of(z * 8, 8), 8)
    for b in range(ROW):
        block = slice(b * BLOCK, (b + 1) * BLOCK)
        xs = pos[0:1, block] * (8.0 * COLS * SPACING)
        ys = pos[1:2, block] * (4.0 * COLS * SPACING)
        level = (tx[0:1, block] - 10.0) * DB
        for ref, values in ((site_x, xs), (site_y, ys), (site_a, level)):
            ref[b] = jnp.transpose(jnp.broadcast_to(values, (BLOCK, BLOCK)))

    lane = lax.broadcasted_iota(jnp.int32, (1, 128), 1)
    column = (j % 2) * 128 + lane
    pixel_row = band * 4 + j // 2

    def path_loss(b):
        @pl.loop(0, 16)
        def _(pair):
            for u in range(2):
                tile = pair * 2 + u
                px = ((tile % 8) * COLS + column).astype(jnp.float32) * SPACING
                py = ((tile // 8) * COLS + pixel_row).astype(jnp.float32) * SPACING
                dx = site_x[b] - px
                dy = site_y[b] - py
                d2 = dx * dx + dy * dy + SPACING * SPACING
                loss[pair, b * BLOCK : (b + 1) * BLOCK, u * 128 : (u + 1) * 128] = (
                    site_a[b] - (1.1 / math.log(2.0)) * jnp.log(d2)
                )

    def split_candidates():
        for b in range(ROW):
            ids = jnp.broadcast_to(cbuf[b, 0:1, :], (BLOCK, BLOCK))
            place = lax.broadcasted_iota(jnp.int32, (BLOCK, BLOCK), 0).astype(jnp.float32)
            hit = jnp.max(jnp.where(ids == place, 1.0, 0.0), axis=1, keepdims=True)
            is_cand = jnp.broadcast_to(hit, (BLOCK, BLOCK)) > 0.5
            where = (z * 4 + b // 2, slice(b * BLOCK, (b + 1) * BLOCK), slice((b % 2) * 128, (b % 2) * 128 + 128))
            level = loss[where]
            cand_loss[b] = jnp.where(is_cand, level, NOTHING)
            loss[where] = jnp.where(is_cand, NOTHING, level)

    def turn(source, block, p, row):
        half, first, count = PIECES[p]
        if count == 8:
            if first % 16 == 0:
                return
            first, count = first - 8, 16
        values = source[block, first : first + count, half * 16 : half * 16 + 16, :].astype(jnp.float32)
        turned = jnp.transpose(values, (1, 0, 2)).astype(jnp.bfloat16)
        for t in range(16):
            mixed_in[
                half * 8 + t // 2,
                row * BLOCK + first : row * BLOCK + first + count,
                (t % 2) * 128 : (t % 2) * 128 + 128,
            ] = turned[t]

    def mix(half, b):
        w = wbuf[b % 2, b // 2]

        @pl.loop(0, 8, unroll=8)
        def _(step):
            pair = half * 8 + step
            fresh = mixed_in[pair, b * BLOCK : (b + 4) * BLOCK, :]
            mixed = jnp.dot(w, fresh, preferred_element_type=jnp.float32)
            power = jnp.exp2(loss[pair, b * BLOCK : (b + 1) * BLOCK, :] + FIELD_GAIN * mixed)
            added = jnp.sum(power.reshape(BLOCK // 8, 8, 256), axis=0)
            acc[2 * pair, 0] += added[:, :128]
            acc[2 * pair + 1, 0] += added[:, 128:]

    acc[...] = jnp.zeros_like(acc)

    @pl.when(z == 0)
    def _():
        mixed_in[:, 0 : HALO * BLOCK, :] = jnp.zeros((16, HALO * BLOCK, 256), jnp.bfloat16)

    def halo_in(p):
        @pl.when(z > 0)
        def _():
            for h in range(HALO):
                forward(h, p).wait_recv()
                turn(halo, h, p, h)

    first_half = [p for p in range(PARTS) if PIECES[p][0] == 0]
    second_half = [p for p in range(PARTS) if PIECES[p][0] == 1]
    loss_blocks = {p: [b for b in range(ROW) if b * 3 // ROW == p] for p in range(3)}

    def serve(blocks):
        for b in blocks:
            tile = z * 8 + b
            lanes = slice((b % 2) * 128, (b % 2) * 128 + 128)
            fresh = mixed_in[z * 4 + b // 2, b * BLOCK : (b + 4) * BLOCK, lanes]
            mixed = jnp.dot(wbuf[b % 2, b // 2], fresh, preferred_element_type=jnp.float32)
            level = cand_loss[b]
            power = jnp.exp2(level + FIELD_GAIN * mixed)
            best = jnp.max(power, axis=0, keepdims=True)
            serves = (power == best) & (level > 0.5 * NOTHING)
            ties = jnp.sum(jnp.where(serves, 1.0, 0.0), axis=0, keepdims=True)
            rest = jnp.sum(jnp.where(serves, 0.0, power), axis=0, keepdims=True)
            acc[tile, 0, 0:1, :] += rest + jnp.where(ties > 1.5, (ties - 1.0) * best, 0.0)
            acc[tile, 1, 0:1, :] = best

    def o_copy(to_z, q):
        owner = to_z * 8 + (at_row(*PEERS[q]) if q < 7 else j)
        return remote(
            acc.at[owner], rows.at[z, j], o_send.at[0], o_recv.at[0], owner, band
        )

    def hand_over(half):
        for q in range(8):
            for to_z in (2 * half, 2 * half + 1):
                if q < 7:
                    o_copy(to_z, q).start()
                else:
                    @pl.when(to_z != z)
                    def _():
                        o_copy(to_z, q).start()

    def sent(p):
        sites, tiles = piece(p)
        seven = land.at[pl.ds(0, 7), sites, tiles]
        pltpu.make_async_copy(seven, seven, send_sem.at[p]).wait()

    def forwarded(pieces):
        @pl.when(z < 3)
        def _():
            for p in pieces:
                for h in range(HALO):
                    forward(h, p).wait_send()

    def pass_on(p):
        for h in (1, 2, 0):
            arrived(ROW - HALO + h, p)

            @pl.when(z < 3)
            def _():
                forward(h, p).start()

        if HELD and p == TRIGGER:
            @pl.when(j < 4)
            def _():
                for k in range(PARTS - HELD, PARTS):
                    for q in HELD_TO:
                        send(q, k).start()

    for p in range(PARTS - HELD):
        pass_on(p)
        for b in loss_blocks.get(p, ()):
            path_loss(b)
        if p == 0:
            for dx in (1, 2, 3):
                other = (x + dx) % 4
                got = wbuf.at[c, other, quarter]
                pltpu.make_async_copy(got, got, w_recv.at[other]).wait()
            for dc in (0, 1):
                for dy in range(4):
                    if dc or dy:
                        w2_copy(dc, dy).start()
        if p == 1:
            for q in range(7):
                other = at_row(*PEERS[q])
                pltpu.make_async_copy(cbuf.at[other], cbuf.at[other], c_recv.at[other]).wait()
            for dc in (0, 1):
                for dy in range(4):
                    if dc or dy:
                        other_c, other_y = (c + dc) % 2, (band + dy) % 4
                        got = wbuf.at[other_c, :, pl.ds(pl.multiple_of(other_y * 32, 32), 32)]
                        pltpu.make_async_copy(got, got, w2_recv.at[other_c * 4 + other_y]).wait()
        if p == 2:
            split_candidates()
        for b in range(ROW):
            if b < ROW - HALO:
                arrived(b, p)
            turn(land, b, p, b + HALO)
        if p == first_half[-1]:
            for b in range(HALO, ROW):
                mix(0, b)
        if p == second_half[1]:
            for k in first_half:
                halo_in(k)
            for b in range(HALO):
                mix(0, b)

            @pl.when(z < 2)
            def _():
                serve(range(ROW))

            hand_over(0)
        if p == 3:
            for q in range(7):
                c_copy(q).wait_send()
            for dx in (1, 2, 3):
                w_copy(dx).wait_send()
            for dc in (0, 1):
                for dy in range(4):
                    if dc or dy:
                        w2_copy(dc, dy).wait_send()
        if p >= 2:
            sent(p - 2)
    held = range(PARTS - HELD, PARTS)
    for p in held:
        pass_on(p)
        for b in range(ROW - HALO, ROW):
            turn(land, b, p, b + HALO)
    late = held if HELD else (PARTS - 2, PARTS - 1)
    for k in second_half:
        if k not in late:
            halo_in(k)
    for p in range(PARTS - HELD - 2, PARTS - HELD):
        sent(p)
    forwarded(range(PARTS - HELD))
    for p in held:
        arrived(4, p)
        turn(land, 4, p, 4 + HALO)
    mix(1, 7)
    for p in held:
        for b in range(4):
            arrived(b, p)
            turn(land, b, p, b + HALO)
    for b in range(HALO, ROW - 1):
        mix(1, b)

    @pl.when(z >= 2)
    def _():
        serve(range(HALO, ROW))

    for p in held:
        sent(p)
    forwarded(held)
    for p in late:
        halo_in(p)
    for b in range(HALO):
        mix(1, b)

    @pl.when(z >= 2)
    def _():
        serve(range(HALO))

    hand_over(1)
    pltpu.make_async_copy(acc.at[site], rows.at[z, j], o_recv.at[0]).start()
    pltpu.make_async_copy(rows, rows, o_recv.at[0]).wait()
    others = jnp.sum((rows[0, :, 0] + rows[1, :, 0]) + (rows[2, :, 0] + rows[3, :, 0]), axis=1)
    best = jnp.max(rows[z, :, 1], axis=1)
    to_log10 = 1.0 / math.log(10.0)
    best_level = jnp.log(best) * to_log10
    sinr_level = jnp.log(best / others) * to_log10
    total = jnp.sum(sinr_level, axis=0, keepdims=True)
    msum[...] = jnp.broadcast_to(total, (8, 128))

    def m_copy(dy):
        return remote(msum, means.at[band], m_send.at[dy], m_recv.at[band], site, (band + dy) % 4)

    for dy in (1, 2, 3):
        m_copy(dy).start()
    means[band] = msum[...]
    out[0:8, :] = best_level
    out[8:16, :] = sinr_level
    for dy in (1, 2, 3):
        came = (band + dy) % 4
        pltpu.make_async_copy(means.at[came], means.at[came], m_recv.at[came]).wait()
    total = (means[0] + means[1]) + (means[2] + means[3])
    mean = jnp.sum(total, axis=1, keepdims=True) * (1.0 / 4096.0)
    out[16:24, :] = jnp.broadcast_to(mean, (8, 128))

    handed = acc.at[pl.ds(0, 31)]
    pltpu.make_async_copy(handed, handed, o_send.at[0]).wait()
    for dx in (1, 2, 3):
        m_copy(dx).wait_send()


def hand_out(out, best, sinr, mean):
    for k in range(8):
        best[:, k * 128 : (k + 1) * 128] = out[k : k + 1, :]
        sinr[:, k * 128 : (k + 1) * 128] = out[8 + k : 9 + k, :]
    mean[...] = out[16:17, :]


def shards(fields, factor, pattern, tx_power, site_position, candidates):
    dma = pltpu.SemaphoreType.DMA
    f32, bf16 = jnp.float32, jnp.bfloat16
    vmem = pl.BlockSpec(memory_space=pltpu.VMEM)
    out = pl.pallas_call(
        kernel,
        out_shape=pltpu.VMEM((24, 128), f32),
        in_specs=[pl.BlockSpec(memory_space=pl.ANY)] * 6,
        out_specs=vmem,
        scratch_shapes=[
            pltpu.VMEM((32, 4, BLOCK), bf16),
            pltpu.VMEM((1, 3), jnp.int32),
            pltpu.VMEM((1, 1024), f32),
            pltpu.VMEM((2, 1024), f32),
            pltpu.VMEM((1, 16), jnp.int32),
            pltpu.VMEM((ROW, BLOCK, 32, 128), bf16),
            pltpu.VMEM((HALO, BLOCK, 32, 128), bf16),
            pltpu.VMEM((16, (HALO + ROW) * BLOCK, 256), bf16),
            pltpu.VMEM((16, ROW * BLOCK, 256), f32),
            pltpu.VMEM((ROW, BLOCK, 128), f32),
            pltpu.VMEM((2, 4, BLOCK, 512), bf16),
            pltpu.VMEM((ROW, BLOCK, 128), f32),
            pltpu.VMEM((ROW, BLOCK, 128), f32),
            pltpu.VMEM((ROW, BLOCK, 128), f32),
            pltpu.VMEM((ROW, 8, 128), f32),
            pltpu.VMEM((32, 2, 8, 128), f32),
            pltpu.VMEM((4, ROW, 2, 8, 128), f32),
            pltpu.VMEM((8, 128), f32),
            pltpu.VMEM((4, 8, 128), f32),
            dma((PARTS,)), dma((8 * PARTS,)), dma((HALO * PARTS,)), dma((HALO * PARTS,)),
            dma((4,)), dma((4,)), dma((8,)), dma((8,)), dma((7,)), dma((8,)),
            dma((1,)), dma((1,)), dma((4,)), dma((4,)), dma((5,)),
        ],
        compiler_params=pltpu.CompilerParams(
            collective_id=0, has_side_effects=True, vmem_limit_bytes=56 << 20
        ),
    )(fields, factor, pattern, tx_power.reshape(1, -1), site_position, candidates)
    best, sinr, mean = pl.pallas_call(
        hand_out,
        out_shape=(
            jax.ShapeDtypeStruct((1, 1024), f32),
            jax.ShapeDtypeStruct((1, 1024), f32),
            jax.ShapeDtypeStruct((1, 128), f32),
        ),
        in_specs=[vmem],
        out_specs=(vmem, vmem, vmem),
    )(out)
    return (best, sinr, mean[0, 0:1])


def solution(mesh):
    placed = (
        P("site", None, "band"),
        P("site", None, None),
        P("site", None),
        P(),
        P(),
        P("site", None),
    )
    return jax.shard_map(
        shards,
        mesh=mesh,
        in_specs=placed,
        out_specs=(P("site", "band"), P("site", "band"), P("site")),
        check_vma=False,
    )
```
